128 devices in a mesh: section: 2 (over x_hi), dp: 32 (over z, y, x_lo), mp: 2 (over core).
Axes of the slice: x: 4 (x_hi: 2, x_lo: 2; x = x_hi * 2 + x_lo), y: 4, z: 4, core: 2. Of those that a mesh axis runs over, the one named last changes fastest.
Arguments:
- saved_input: bfloat16 [2, 2, 8192, 4096], P('section', None, 'dp', 'mp')
- out_grad: bfloat16 [2, 8192, 4096], P(None, 'dp', 'mp'), may hold values from -6 to 6
- master_weight: float32 [2, 4096, 4096], P('section', 'mp', 'dp'), may hold values from -0.09375 to 0.09375
- moment1: float32 [2, 4096, 4096], P('section', 'mp', 'dp'), may hold values from -2 to 2
- moment2: float32 [2, 4096, 4096], P('section', 'mp', 'dp'), may hold values from 0.01 to 1
Outputs:
- input_grad: bfloat16 [2, 2, 8192, 4096], P('section', None, 'dp', 'mp')
- new_weight: float32 [2, 4096, 4096], P('section', 'mp', 'dp')
- new_moment1: float32 [2, 4096, 4096], P('section', 'mp', 'dp')
- new_moment2: float32 [2, 4096, 4096], P('section', 'mp', 'dp')
The draws below stay inside these ranges and needn't reach their ends.
All inputs are finite; a program needn't handle non-finite values.
Results may differ from the reference program's by a relative error of at most 0.0054.
Values may be sent and summed in bfloat16 or wider, within the bound.
A program may use at most 256 MiB of HBM per device.

```python
import math
import jax
import jax.numpy as jnp

D = 4096
TOK_DEV = 256
MB = 2
SECTIONS = 2
TOKENS = 8192


def block_scales(key, count, length, spread):
    levels = jnp.exp(jax.random.uniform(key, (count,), jnp.float32, 0.0, math.log(spread)))
    return jnp.repeat(levels, length)


def draw_saved_input(key, part):
    key = jax.random.fold_in(key, 7)
    key_rows, key_columns, key_values = jax.random.split(key, 3)
    shape = (SECTIONS, MB, TOKENS, D)
    spread = 10.0
    values = jax.random.normal(key_values, shape, jnp.float32)
    row_length = TOK_DEV // 8
    row_scale = block_scales(key_rows, SECTIONS * MB * TOKENS // row_length, row_length, spread)
    column_scale = block_scales(key_columns, SECTIONS * 64, D // 64, spread)
    rows = row_scale.reshape(SECTIONS, MB, TOKENS, 1)
    columns = column_scale.reshape(SECTIONS, 1, 1, D)
    return (values * rows * columns).astype(jnp.bfloat16)


def shard_levels(rng, extent, cuts, smallest, high):
    gain = 1.0
    for position, blocks in cuts:
        heights = jax.random.uniform(jax.random.fold_in(jax.random.fold_in(rng, 6), position), (blocks,), jnp.float32, smallest / len(cuts), high / len(cuts))
        gain = gain * jnp.repeat(jnp.exp(heights), extent[position] // blocks).reshape((-1,) + (1,) * (len(extent) - 1 - position))
    return gain


def scatter_about(rng, dims, scale, most, cuts=(), dtype=jnp.bfloat16):
    gain = shard_levels(rng, dims, cuts, -0.22, 0.18) if cuts else 1.0
    values = jax.random.normal(rng, dims, jnp.float32) * scale * gain
    return jnp.minimum(jnp.maximum(values, -most), most).astype(dtype)


def setup_inputs(seed: int = 0) -> dict:
    seeds = jax.random.split(jax.random.key(seed), 6)
    return {
        "saved_input": draw_saved_input(jax.random.fold_in(seeds[5], 71), 0),
        "out_grad": scatter_about(seeds[1], (MB, TOKENS, D), 1.0, 6.0, ((1, 32), (2, 2))),
        "master_weight": scatter_about(seeds[2], (SECTIONS, D, D), D ** -0.5, 0.09375, ((0, 2), (1, 2), (2, 32)), jnp.float32),
        "moment1": scatter_about(seeds[3], (SECTIONS, D, D), 0.3, 2.0, ((0, 2), (1, 2), (2, 32)), jnp.float32),
        "moment2": jnp.clip(jnp.exp(math.log(1.0) - 4.6051702 * jax.random.uniform(seeds[4], (SECTIONS, D, D), jnp.float32) ** shard_levels(seeds[4], (SECTIONS, D, D), ((0, 2), (1, 2), (2, 32)), -0.2, 0.2)), 0.01, 1.0),
    }


def reference(saved_input, out_grad, master_weight, moment1, moment2):
    weight_bf = master_weight.astype(jnp.bfloat16)
    grad_in = out_grad
    input_list = []
    grad_list = []
    for section_index in range(SECTIONS - 1, -1, -1):
        weight_now = weight_bf[section_index].astype(jnp.float32)
        grad_float = grad_in.astype(jnp.float32)
        backward_term = jnp.einsum('mtj,ij->mti', grad_float, weight_now)
        layer_grad = (grad_float + backward_term).astype(jnp.bfloat16)
        inputs_float = saved_input[section_index].astype(jnp.float32)
        weight_grad = jnp.einsum('mti,mtj->ij', inputs_float, grad_float)
        input_list.insert(0, layer_grad)
        grad_list.insert(0, weight_grad)
        grad_in = layer_grad
    input_grad = jnp.stack(input_list)
    grads = jnp.stack(grad_list)
    total_squares = jnp.sum(grads * grads)
    rms_value = jnp.sqrt(total_squares / (SECTIONS * D * D))
    clip_factor = jnp.minimum(1.0, 1.0 / (rms_value + 1e-06))
    clipped = clip_factor * grads
    new_moment1 = 0.9 * moment1 + 0.1 * clipped
    new_moment2 = 0.95 * moment2 + 0.05 * clipped * clipped
    first_fix = 1.0 - 0.9 ** 10
    second_fix = 1.0 - 0.95 ** 10
    update = new_moment1 / first_fix / (jnp.sqrt(new_moment2 / second_fix) + 1e-08)
    new_weight = master_weight - 0.01 * (update + 0.1 * master_weight)
    return (input_grad, new_weight, new_moment1, new_moment2)
```

```python
import jax
import jax.numpy as jnp
from jax import lax
from jax.experimental import pallas as pl
from jax.experimental.pallas import tpu as pltpu
from jax.sharding import PartitionSpec as P

MESH = pl.DeviceIdType.MESH
BF = jnp.bfloat16
F32 = jnp.float32
W_X, X_X, G_X, G_CUT, G_CORE, G_CORE2, G_CORE3, D_CUT, D_CORE, P_X, O_X, F_X = 0, 1, 2, 3, 4, 5, 6, 7, 11, 15, 19, 20


def dot_nt(a, b):
    return lax.dot_general(a, b, (((1,), (1,)), ((), ())), preferred_element_type=F32)


def dot_nn(a, b):
    return jnp.dot(a, b, preferred_element_type=F32)


def kernel(
    x_hbm, g_hbm, w_ref, out_ref, grad_ref, total_ref,
    Wg, Wx, Gv, D, Dp, Xo, Xp, XT, S, R1, R2, T, Tf, F, Fp, acc, Nb,
    ldx, ldg, ag_s, ag_r, rs_s, rs_r, ms, mr, ns, nr,
):
    s = lax.axis_index("section")
    d = lax.axis_index("dp")
    c = lax.axis_index("mp")
    z, y, p = d // 8, (d // 2) % 4, d % 2
    u = jnp.where(s == 1, 1 - p, p)

    def dev(s_, z_, y_, p_, c_):
        return (s_, (z_ * 4 + y_) * 2 + p_, c_)

    def zdev(o):
        return dev(s, (z + o) % 4, y, p, c)

    def ydev(o):
        return dev(s, z, (y + o) % 4, p, c)

    pair = dev(s, z, y, 1 - p, c)
    cut = dev(1 - s, z, y, 1 - p, c)
    core = dev(s, z, y, p, 1 - c)
    above = s == 1
    below = s == 0

    def rc(src, dst, i, to):
        return pltpu.make_async_remote_copy(src, dst, ms.at[i], mr.at[i], device_id=to, device_id_type=MESH)

    def xload(i):
        return pltpu.make_async_copy(x_hbm.at[:, pl.ds(128 * i, 128)], Xo.at[i // 2, i % 2], ldx.at[i])

    def gload(i, dst):
        return pltpu.make_async_copy(g_hbm.at[:, pl.ds(256 * i, 256)], dst, ldg.at[i])

    for i in range(16):
        xload(i).start()

    @pl.when(above)
    def _():
        for i in range(8):
            gload(i, Gv.at[p, 8 * c + i]).start()

    @pl.when(below)
    def _():
        for i in range(4, 8):
            gload(i, Gv.at[0, 8 + i]).start()

    @pl.when(above)
    def _():
        for r in range(8):
            Wg[z, y, p, 128 * r : 128 * r + 128] = w_ref[pl.ds(256 * r + 128 * u, 128), :].astype(BF)
            Wx[128 * r : 128 * r + 128] = w_ref[pl.ds(256 * r + 128 * (1 - u), 128), :].astype(BF)

    @pl.when(below)
    def _():
        for r in range(8):
            Wg[z, y, r // 4, 256 * (r % 4) : 256 * (r % 4) + 256] = w_ref[256 * r : 256 * r + 256, :].astype(BF)

    barrier = pltpu.get_barrier_semaphore()
    peers = [zdev(1), zdev(2), zdev(3), ydev(1), ydev(2), ydev(3), pair, cut, core]
    for to in peers:
        pl.semaphore_signal(barrier, inc=1, device_id=to, device_id_type=MESH)
    pl.semaphore_wait(barrier, len(peers))

    w_x = rc(Wx, Wg.at[z, y, p], W_X, pair)
    w_x_in = rc(Wx, Wg.at[z, y, 1 - p], W_X, pair)
    g_x = rc(Gv.at[p, pl.ds(8 * c, 4)], Gv.at[p, pl.ds(8 * c, 4)], G_X, pair)
    g_x_in = rc(Gv.at[1 - p, pl.ds(8 * c, 4)], Gv.at[1 - p, pl.ds(8 * c, 4)], G_X, pair)
    g_cut = rc(Gv.at[0, pl.ds(12, 4)], Gv.at[p, pl.ds(8 * c + 4, 4)], G_CUT, cut)
    g_cut_in = rc(Gv.at[1 - p, pl.ds(8 * c + 4, 4)], Gv.at[1 - p, pl.ds(8 * c + 4, 4)], G_CUT, cut)
    g_core = rc(Gv.at[p, pl.ds(8 * c, 8)], Gv.at[p, pl.ds(8 * c, 8)], G_CORE, core)
    g_core_in = rc(Gv.at[p, pl.ds(8 * (1 - c), 8)], Gv.at[p, pl.ds(8 * (1 - c), 8)], G_CORE, core)
    g_core2 = rc(Gv.at[1 - p, pl.ds(8 * c, 4)], Gv.at[1 - p, pl.ds(8 * c, 4)], G_CORE2, core)
    g_core2_in = rc(Gv.at[1 - p, pl.ds(8 * (1 - c), 4)], Gv.at[1 - p, pl.ds(8 * (1 - c), 4)], G_CORE2, core)
    g_core3 = rc(Gv.at[1 - p, pl.ds(8 * c + 4, 4)], Gv.at[1 - p, pl.ds(8 * c + 4, 4)], G_CORE3, core)
    g_core3_in = rc(Gv.at[1 - p, pl.ds(8 * (1 - c) + 4, 4)], Gv.at[1 - p, pl.ds(8 * (1 - c) + 4, 4)], G_CORE3, core)
    x_half = rc(Xo.at[:, 1 - u], Xp.at[:, 1 - u], X_X, pair)
    x_half_in = rc(Xo.at[:, u], Xp.at[:, u], X_X, pair)
    x_full = rc(Xo, Xp, X_X, pair)

    def ag1(k, h, o):
        block = Wg.at[z, y, h, pl.ds(256 * k, 256)]
        return pltpu.make_async_remote_copy(
            block, block, ag_s.at[0, k, h, o - 1], ag_r.at[0, k, h, o - 1],
            device_id=zdev(o) if h == 0 else ydev(o), device_id_type=MESH)

    def ag2(k, h, o):
        row = Wg.at[:, y, h, pl.ds(256 * k, 256)] if h == 0 else Wg.at[z, :, h, pl.ds(256 * k, 256)]
        return pltpu.make_async_remote_copy(
            row, row, ag_s.at[1, k, h, o - 1], ag_r.at[1, k, h, o - 1],
            device_id=ydev(o) if h == 0 else zdev(o), device_id_type=MESH)

    @pl.when(above)
    def _():
        w_x.start()
        for i in range(8):
            gload(i, Gv.at[p, 8 * c + i]).wait()
        g_core.start()
        g_x.start()
        w_x_in.wait_recv()

    @pl.when(below)
    def _():
        for i in range(4, 8):
            gload(i, Gv.at[0, 8 + i]).wait()
        g_cut.start()

    @pl.loop(0, 4)
    def _(k):
        for h in range(2):
            for o in (1, 3, 2):
                ag1(k, h, o).start()

    for i in range(16):
        xload(i).wait()

    @pl.when(above)
    def _():
        x_half.start()

    @pl.when(below)
    def _():
        x_full.start()

    @pl.loop(0, 4)
    def _(k):
        for h in range(2):
            for o in (1, 3, 2):
                ag1(k, h, o).wait_recv()
            for o in (1, 3, 2):
                ag2(k, h, o).start()

    @pl.when(above)
    def _():
        @pl.loop(0, 8)
        def _(r):
            XT[pl.ds(128 * r, 128), pl.ds(512 * p, 512)] = Xo[r, u].T

    @pl.when(below)
    def _():
        @pl.loop(0, 16)
        def _(i):
            XT[pl.ds(128 * i, 128), pl.ds(512 * p, 512)] = Xo[i // 2, i % 2].T

    @pl.when(above)
    def _():
        g_x_in.wait_recv()
        g_core2.start()
        g_cut_in.wait_recv()
        g_core3.start()
        g_core_in.wait_recv()
        g_core2_in.wait_recv()
        g_core3_in.wait_recv()

        @pl.loop(0, 4)
        def _(k):
            for h in range(2):
                for o in (1, 3, 2):
                    ag2(k, h, o).wait_recv()

            @pl.loop(0, 2)
            def _(t):
                for zz in range(4):
                    left = jnp.concatenate([Gv[t, 4 * zz + yy] for yy in range(4)], axis=1)
                    right = jnp.concatenate(
                        [Wg[zz, yy, h, pl.ds(256 * k, 256), :] for yy in range(4) for h in range(2)], axis=1)
                    part = dot_nt(left, right)
                    acc[...] = part if zz == 0 else acc[...] + part
                for rr in range(2):
                    q = 8 * c + 2 * k + rr
                    mine = Gv[t, q, :, pl.ds(128 * u, 128)].astype(F32)
                    D[q, pl.ds(512 * t, 512)] = (acc[:, 128 * rr : 128 * rr + 128] + mine).astype(BF)

            out = D.at[pl.ds(8 * c + 2 * k, 2)]
            rc(out, out, D_CUT + k, cut).start()

        rc(D.at[pl.ds(8 * c, 8), pl.ds(512 * (1 - p), 512)], Dp, O_X, pair).start()
        x_half_in.wait_recv()

        @pl.loop(0, 8)
        def _(r):
            XT[pl.ds(128 * r, 128), pl.ds(512 * (1 - p), 512)] = Xp[r, u].T

    @pl.when(below)
    def _():
        x_full.wait_recv()

        @pl.loop(0, 16)
        def _(i):
            XT[pl.ds(128 * i, 128), pl.ds(512 * (1 - p), 512)] = Xp[i // 2, i % 2].T

        @pl.loop(0, 4)
        def _(k):
            for h in range(2):
                for o in (1, 3, 2):
                    ag2(k, h, o).wait_recv()

        @pl.loop(0, 4)
        def _(k):
            got = D.at[pl.ds(8 * c + 2 * k, 2)]
            rc(got, got, D_CUT + k, cut).wait_recv()
            rc(got, got, D_CORE + k, core).start()

        @pl.loop(0, 4)
        def _(k):
            got = D.at[pl.ds(8 * (1 - c) + 2 * k, 2)]
            rc(got, got, D_CORE + k, core).wait_recv()

    def rs1(m, h, o):
        if h == 0:
            src, to = S.at[m, (z + o) % 4, :, h], zdev(o)
        else:
            src, to = S.at[m, :, (y + o) % 4, h], ydev(o)
        return pltpu.make_async_remote_copy(
            src, R1.at[m, h, o - 1], rs_s.at[0, m, h, o - 1], rs_r.at[0, m, h, o - 1],
            device_id=to, device_id_type=MESH)

    def rs2(m, h, o):
        if h == 0:
            src, to = T.at[m, h, (y + o) % 4], ydev(o)
        else:
            src, to = T.at[m, h, (z + o) % 4], zdev(o)
        return pltpu.make_async_remote_copy(
            src, R2.at[m, h, o - 1], rs_s.at[1, m, h, o - 1], rs_r.at[1, m, h, o - 1],
            device_id=to, device_id_type=MESH)

    @pl.loop(0, 4)
    def _(m):
        @pl.when(above)
        def _():
            @pl.loop(0, 16)
            def _(q):
                v = dot_nn(XT[pl.ds(256 * m, 256), 0:512], Gv[0, q])
                v = v + dot_nn(XT[pl.ds(256 * m, 256), 512:1024], Gv[1, q])
                S[m, q // 4, q % 4, 0] = v[:, :128].astype(BF)
                S[m, q // 4, q % 4, 1] = v[:, 128:].astype(BF)

        @pl.when(below)
        def _():
            @pl.loop(0, 16)
            def _(i):
                h, q = i // 8, 2 * (i % 8)
                right = jnp.concatenate([D[q], D[q + 1]], axis=1)
                v = dot_nn(XT[pl.ds(1024 * h + 256 * m, 256), 0:1024], right)
                S[m, q // 4, q % 4, h] = v[:, :128].astype(BF)
                S[m, q // 4, q % 4 + 1, h] = v[:, 128:].astype(BF)

        for h in range(2):
            for o in (1, 3, 2):
                rs1(m, h, o).start()

    def input_part(n, t):
        for zz in range(4):
            left = jnp.concatenate([D[4 * zz + yy, pl.ds(512 * t, 512)] for yy in range(4)], axis=1)
            right = jnp.concatenate(
                [Wg[zz, yy, n // 4, pl.ds(256 * (n % 4), 256), :] for yy in range(4)], axis=1)
            part = dot_nt(left, right)
            acc[...] = part if zz == 0 else acc[...] + part
        lanes = pl.ds(128 * p, 128)
        acc[:, lanes] = acc[:, lanes] + D[8 * c + n, pl.ds(512 * t, 512)].astype(F32)

    def p_x(i):
        return rc(Gv.at[0, pl.ds(2 * i, 2)], Gv.at[1, pl.ds(2 * i, 2)], P_X + i, pair)

    @pl.when(below)
    def _():
        @pl.loop(0, 4)
        def _(i):
            @pl.loop(0, 2)
            def _(j):
                input_part(2 * i + j, 1 - p)
                Gv[0, 2 * i + j] = acc[...].astype(BF)

            p_x(i).start()

    @pl.loop(0, 4)
    def _(m):
        for h in range(2):
            for o in (1, 3, 2):
                rs1(m, h, o).wait_recv()

            @pl.loop(0, 4)
            def _(b):
                own = S[m, z, b, h] if h == 0 else S[m, b, y, h]
                v = own.astype(F32)
                for o in range(3):
                    v = v + R1[m, h, o, b].astype(F32)
                T[m, h, b] = v.astype(BF)

                @pl.when(b == (y if h == 0 else z))
                def _():
                    Tf[m, h] = v

            for o in (1, 3, 2):
                rs2(m, h, o).start()

    @pl.when(below)
    def _():
        @pl.loop(0, 4)
        def _(i):
            p_x(i).wait_recv()

            @pl.loop(0, 2)
            def _(j):
                n = 2 * i + j
                input_part(n, p)
                out_ref[:, pl.ds(pl.multiple_of(256 * n, 256), 256)] = (acc[...] + Gv[1, n].astype(F32)).astype(BF)

    @pl.when(above)
    def _():
        rc(Dp, Dp, O_X, pair).wait_recv()

        @pl.loop(0, 8)
        def _(r):
            out_ref[:, pl.ds(256 * r + 128 * u, 128)] = D[8 * c + r, pl.ds(512 * p, 512)]
            out_ref[:, pl.ds(256 * r + 128 * (1 - u), 128)] = Dp[r]

    Nb[0, 0] = jnp.zeros((8, 128), F32)

    @pl.loop(0, 4)
    def _(m):
        for h in range(2):
            for o in (1, 3, 2):
                rs2(m, h, o).wait_recv()
            v = Tf[m, h]
            for o in range(3):
                v = v + R2[m, h, o].astype(F32)
            F[h, 2 * m] = v[:128]
            F[h, 2 * m + 1] = v[128:]
            Nb[0, 0] = Nb[0, 0] + jnp.sum((v * v).reshape(32, 8, 128), axis=0)

    f_x = rc(F.at[1 - p], Fp, F_X, pair)

    @pl.when(above)
    def _():
        f_x.start()

    steps = [[core], [pair], [cut], [ydev(1), ydev(3), ydev(2)], [zdev(1), zdev(3), zdev(2)]]
    for i, targets in enumerate(steps):
        copies = [
            pltpu.make_async_remote_copy(
                Nb.at[i, 0], Nb.at[i, j + 1], ns.at[i, j], nr.at[i, j], device_id=to, device_id_type=MESH)
            for j, to in enumerate(targets)]
        for copy in copies:
            copy.start()
        for copy in copies:
            copy.wait_recv()
        v = Nb[i, 0]
        for j in range(len(targets)):
            v = v + Nb[i, j + 1]
        if i + 1 < len(steps):
            Nb[i + 1, 0] = v
        else:
            total_ref[...] = v
        for copy in copies:
            copy.wait_send()

    @pl.when(above)
    def _():
        f_x.wait_recv()
        for r in range(8):
            grad_ref[2 * r + u] = F[p, r]
            grad_ref[2 * r + 1 - u] = Fp[r]

    @pl.when(below)
    def _():
        for r in range(8):
            grad_ref[r] = F[0, r]
            grad_ref[8 + r] = F[1, r]

    @pl.loop(0, 4)
    def _(k):
        for h in range(2):
            for o in (1, 3, 2):
                ag1(k, h, o).wait_send()
                ag2(k, h, o).wait_send()
                rs1(k, h, o).wait_send()
                rs2(k, h, o).wait_send()

    @pl.when(above)
    def _():
        for copy in (w_x, g_x, g_core, g_core2, g_core3, x_half, f_x):
            copy.wait_send()
        rc(Dp, Dp, O_X, pair).wait_send()

        @pl.loop(0, 4)
        def _(k):
            out = D.at[pl.ds(8 * c + 2 * k, 2)]
            rc(out, out, D_CUT + k, cut).wait_send()

    @pl.when(below)
    def _():
        g_cut.wait_send()
        x_full.wait_send()

        @pl.loop(0, 4)
        def _(k):
            out = D.at[pl.ds(8 * c + 2 * k, 2)]
            rc(out, out, D_CORE + k, core).wait_send()
            p_x(k).wait_send()


def per_device(saved_input, out_grad, master_weight, moment1, moment2):
    vmem = pl.BlockSpec(memory_space=pltpu.VMEM)
    hbm = pl.BlockSpec(memory_space=pl.ANY)
    dma = pltpu.SemaphoreType.DMA
    input_grad, grad, total = pl.pallas_call(
        kernel,
        out_shape=(
            jax.ShapeDtypeStruct((512, 2048), BF),
            jax.ShapeDtypeStruct((16, 128, 128), F32),
            jax.ShapeDtypeStruct((8, 128), F32),
        ),
        in_specs=[hbm, hbm, vmem],
        out_specs=(vmem, vmem, vmem),
        scratch_shapes=[
            pltpu.VMEM((4, 4, 2, 1024, 128), BF),
            pltpu.VMEM((1024, 128), BF),
            pltpu.VMEM((2, 16, 512, 256), BF),
            pltpu.VMEM((16, 1024, 128), BF),
            pltpu.VMEM((8, 512, 128), BF),
            pltpu.VMEM((8, 2, 512, 128), BF),
            pltpu.VMEM((8, 2, 512, 128), BF),
            pltpu.VMEM((2048, 1024), BF),
            pltpu.VMEM((4, 4, 4, 2, 256, 128), BF),
            pltpu.VMEM((4, 2, 3, 4, 256, 128), BF),
            pltpu.VMEM((4, 2, 3, 256, 128), BF),
            pltpu.VMEM((4, 2, 4, 256, 128), BF),
            pltpu.VMEM((4, 2, 256, 128), F32),
            pltpu.VMEM((2, 8, 128, 128), F32),
            pltpu.VMEM((8, 128, 128), F32),
            pltpu.VMEM((512, 256), F32),
            pltpu.VMEM((5, 4, 8, 128), F32),
            dma((16,)), dma((8,)),
            dma((2, 4, 2, 3)), dma((2, 4, 2, 3)),
            dma((2, 4, 2, 3)), dma((2, 4, 2, 3)),
            dma((21,)), dma((21,)),
            dma((5, 3)), dma((5, 3)),
        ],
        compiler_params=pltpu.CompilerParams(
            collective_id=0, has_side_effects=True, vmem_limit_bytes=62 * 2**20),
    )(saved_input.reshape(512, 2048), out_grad.reshape(512, 2048), master_weight[0])
    grad_shard = grad.reshape(2048, 128)
    total_squares = jnp.sum(total)
    rms_value = jnp.sqrt(total_squares / 33554432.0)
    clip_factor = jnp.minimum(1.0, 1.0 / (rms_value + 1e-06))
    clipped = clip_factor * grad_shard
    master = master_weight[0]
    new_moment1 = 0.9 * moment1[0] + 0.1 * clipped
    new_moment2 = 0.95 * moment2[0] + 0.05 * clipped * clipped
    first_fix = 1.0 - 0.9**10
    second_fix = 1.0 - 0.95**10
    update = new_moment1 / first_fix / (jnp.sqrt(new_moment2 / second_fix) + 1e-08)
    new_weight = master - 0.01 * (update + 0.1 * master)
    return (input_grad.reshape(1, 2, 256, 2048), new_weight[None], new_moment1[None], new_moment2[None])


def solution(mesh):
    return jax.shard_map(
        per_device,
        mesh=mesh,
        in_specs=(
            P("section", None, "dp", "mp"),
            P(None, "dp", "mp"),
            P("section", "mp", "dp"),
            P("section", "mp", "dp"),
            P("section", "mp", "dp"),
        ),
        out_specs=(
            P("section", None, "dp", "mp"),
            P("section", "mp", "dp"),
            P("section", "mp", "dp"),
            P("section", "mp", "dp"),
        ),
        check_vma=False,
    )
```

```python
import jax
import jax.numpy as jnp
from jax import lax
from jax.experimental import pallas as pl
from jax.experimental.pallas import tpu as pltpu
from jax.sharding import PartitionSpec as P

MESH = pl.DeviceIdType.MESH
BF = jnp.bfloat16
F32 = jnp.float32
X_X, G_X, G_CUT, G_CORE, G_CORE2, G_CORE3, D_CUT, D_CORE, P_X, O_X, F_X, W_X = 0, 1, 2, 3, 4, 5, 6, 14, 22, 26, 27, 28


def dot_nt(a, b):
    return lax.dot_general(a, b, (((1,), (1,)), ((), ())), preferred_element_type=F32)


def dot_nn(a, b):
    return jnp.dot(a, b, preferred_element_type=F32)


def low_lanes(a, b):
    return jnp.where(lax.broadcasted_iota(jnp.int32, a.shape, 1) < 64, a, pltpu.roll(b, 64, 1))


def high_lanes(a, b):
    return jnp.where(lax.broadcasted_iota(jnp.int32, a.shape, 1) < 64, pltpu.roll(a, 64, 1), b)


def kernel(
    x_hbm, g_hbm, w_ref, out_ref, grad_ref,
    Wg, Wx, Gv, D, Dp, Xo, Xp, XT, S, Ra, Rb, Rc, Rd, T, Tf, F, Fp, acc, Nb,
    ldx, ldg, ag_s, ag_r, rs_s, rs_r, ms, mr, ns, nr,
):
    s = lax.axis_index("section")
    d = lax.axis_index("dp")
    c = lax.axis_index("mp")
    z, y, p = d // 8, (d // 2) % 4, d % 2
    u = jnp.where(s == 1, 1 - p, p)

    def dev(s_, z_, y_, p_, c_):
        return (s_, (z_ * 4 + y_) * 2 + p_, c_)

    def zdev(o):
        return dev(s, (z + o) % 4, y, p, c)

    def ydev(o):
        return dev(s, z, (y + o) % 4, p, c)

    pair = dev(s, z, y, 1 - p, c)
    cut = dev(1 - s, z, y, 1 - p, c)
    core = dev(s, z, y, p, 1 - c)
    near = [core, pair, cut, dev(s, z, y, 1 - p, 1 - c), dev(1 - s, z, y, 1 - p, 1 - c),
            dev(1 - s, z, y, p, c), dev(1 - s, z, y, p, 1 - c)]
    above = s == 1
    below = s == 0

    def rc(src, dst, i, to):
        return pltpu.make_async_remote_copy(src, dst, ms.at[i], mr.at[i], device_id=to, device_id_type=MESH)

    def xload(i):
        return pltpu.make_async_copy(x_hbm.at[:, pl.ds(128 * i, 128)], Xo.at[i // 2, i % 2], ldx.at[i])

    def gload(i, dst):
        return pltpu.make_async_copy(g_hbm.at[:, pl.ds(256 * i, 256)], dst, ldg.at[i])

    for i in range(16):
        xload(i).start()

    @pl.when(above)
    def _():
        for i in range(8):
            gload(i, Gv.at[p, 8 * c + i]).start()

    @pl.when(below)
    def _():
        for i in range(4, 8):
            gload(i, Gv.at[0, 8 + i]).start()

    @pl.when(above)
    def _():
        for a in range(16):
            b, r = a // 8, a % 8
            Wg[z, y, p, 64 * a : 64 * a + 64] = w_ref[pl.ds(256 * r + 128 * u + 64 * b, 64), :].astype(BF)
            Wx[64 * a : 64 * a + 64] = w_ref[pl.ds(256 * r + 128 * (1 - u) + 64 * b, 64), :].astype(BF)

    @pl.when(below)
    def _():
        for r in range(8):
            Wg[z, y, r // 4, 256 * (r % 4) : 256 * (r % 4) + 256] = w_ref[256 * r : 256 * r + 256, :].astype(BF)

    barrier = pltpu.get_barrier_semaphore()
    peers = [zdev(1), zdev(2), zdev(3), ydev(1), ydev(2), ydev(3), *near]
    for to in peers:
        pl.semaphore_signal(barrier, inc=1, device_id=to, device_id_type=MESH)
    pl.semaphore_wait(barrier, len(peers))

    def w_x(k):
        rows = pl.ds(128 * k, 128)
        return rc(Wx.at[rows], Wg.at[z, y, p, rows], W_X + k, pair)

    g_x = rc(Gv.at[p, pl.ds(8 * c, 4)], Gv.at[p, pl.ds(8 * c, 4)], G_X, pair)
    g_x_in = rc(Gv.at[1 - p, pl.ds(8 * c, 4)], Gv.at[1 - p, pl.ds(8 * c, 4)], G_X, pair)
    g_cut = rc(Gv.at[0, pl.ds(12, 4)], Gv.at[p, pl.ds(8 * c + 4, 4)], G_CUT, cut)
    g_cut_in = rc(Gv.at[1 - p, pl.ds(8 * c + 4, 4)], Gv.at[1 - p, pl.ds(8 * c + 4, 4)], G_CUT, cut)
    g_core = rc(Gv.at[p, pl.ds(8 * c, 8)], Gv.at[p, pl.ds(8 * c, 8)], G_CORE, core)
    g_core_in = rc(Gv.at[p, pl.ds(8 * (1 - c), 8)], Gv.at[p, pl.ds(8 * (1 - c), 8)], G_CORE, core)
    g_core2 = rc(Gv.at[1 - p, pl.ds(8 * c, 4)], Gv.at[1 - p, pl.ds(8 * c, 4)], G_CORE2, core)
    g_core2_in = rc(Gv.at[1 - p, pl.ds(8 * (1 - c), 4)], Gv.at[1 - p, pl.ds(8 * (1 - c), 4)], G_CORE2, core)
    g_core3 = rc(Gv.at[1 - p, pl.ds(8 * c + 4, 4)], Gv.at[1 - p, pl.ds(8 * c + 4, 4)], G_CORE3, core)
    g_core3_in = rc(Gv.at[1 - p, pl.ds(8 * (1 - c) + 4, 4)], Gv.at[1 - p, pl.ds(8 * (1 - c) + 4, 4)], G_CORE3, core)
    x_half = rc(Xo.at[:, 1 - u], Xp.at[:, 1 - u], X_X, pair)
    x_half_in = rc(Xo.at[:, u], Xp.at[:, u], X_X, pair)
    x_full = rc(Xo, Xp, X_X, pair)

    def axis(stage, h):
        return (z, zdev) if stage == h else (y, ydev)

    def gather(stage, i, k, h):
        e, to = axis(stage, h)
        e = (e, e, (e + 3) % 4, (e + 1) % 4)[i]
        rows = pl.ds(128 * k + (0, 0, 0, 64)[i], (128, 128, 64, 64)[i])
        if stage == 0:
            ref = Wg.at[e, y, h, rows] if h == 0 else Wg.at[z, e, h, rows]
        else:
            ref = Wg.at[:, e, h, rows] if h == 0 else Wg.at[e, :, h, rows]
        return pltpu.make_async_remote_copy(
            ref, ref, ag_s.at[stage, k, h, i], ag_r.at[stage, k, h, i],
            device_id=to((1, 3, 1, 3)[i]), device_id_type=MESH)

    def gather_on(stage, k):
        for h in range(2):
            for i in range(2):
                gather(stage, i, k, h).wait_recv()
                gather(stage, i + 2, k, h).start()

    def gather_end(stage, k):
        for h in range(2):
            for i in (2, 3):
                gather(stage, i, k, h).wait_recv()

    @pl.when(above)
    def _():
        for k in range(8):
            w_x(k).start()
        for i in range(8):
            gload(i, Gv.at[p, 8 * c + i]).wait()
        g_x.start()
        g_core.start()

    @pl.when(below)
    def _():
        for i in range(4, 8):
            gload(i, Gv.at[0, 8 + i]).wait()
        g_cut.start()

    def gather_begin(k):
        @pl.when(above)
        def _():
            w_x(k).wait_recv()

        for h in range(2):
            for i in range(2):
                gather(0, i, k, h).start()

    def gather_rows(k):
        for h in range(2):
            for i in range(2):
                gather(1, i, k, h).start()

    def unit(k, j):
        t = jnp.where(s == 1, p, 1 - p) if j == 0 else jnp.where(s == 1, 1 - p, p)
        return t, D.at[pl.ds(8 * c + 2 * k, 2), pl.ds(512 * t, 512)]

    def from_core(k, j):
        t = unit(k, j)[0]
        return D.at[pl.ds(8 * (1 - c) + 2 * k, 2), pl.ds(512 * t, 512)]

    def d_cut(k, j):
        ref = unit(k, j)[1]
        return rc(ref, ref, D_CUT + 2 * k + j, cut)

    def d_core(k, j):
        ref = unit(k, j)[1]
        return rc(ref, ref, D_CORE + 2 * k + j, core)

    def d_core_in(k, j):
        ref = from_core(k, j)
        return rc(ref, ref, D_CORE + 2 * k + j, core)

    def d_on(k, j):
        d_cut(k, j).wait_recv()
        d_core(k, j).start()

    def layer_unit(k, j):
        t = unit(k, j)[0]
        for zz in range(4):
            left = jnp.concatenate([Gv[t, 4 * zz + yy] for yy in range(4)], axis=1)
            right = jnp.concatenate(
                [Wg[zz, yy, h, pl.ds(256 * k, 256), :] for yy in range(4) for h in range(2)], axis=1)
            part = dot_nt(left, right)
            acc[...] = part if zz == 0 else acc[...] + part
        for rr in range(2):
            q = 8 * c + 4 * (k % 2) + 2 * rr
            g0 = Gv[t, q, :, pl.ds(128 * u, 128)].astype(F32)
            g1 = Gv[t, q + 1, :, pl.ds(128 * u, 128)].astype(F32)
            mine = jnp.where(k < 2, low_lanes(g0, g1), high_lanes(g0, g1))
            D[8 * c + 2 * k + rr, pl.ds(512 * t, 512)] = (acc[:, 128 * rr : 128 * rr + 128] + mine).astype(BF)
        d_cut(k, j).start()

    gather_begin(0)
    gather_begin(1)

    @pl.loop(0, 12)
    def _(i):
        @pl.when(i < 6)
        def _():
            gather_begin(i + 2)

        @pl.when(i < 8)
        def _():
            gather_on(0, i)

        @pl.when((i >= 1) & (i < 9))
        def _():
            gather_end(0, i - 1)
            gather_rows(i - 1)

        @pl.when((i >= 3) & (i < 11))
        def _():
            gather_on(1, i - 3)

        @pl.when(i >= 4)
        def _():
            gather_end(1, i - 4)

        @pl.when(i == 4)
        def _():
            for j in range(16):
                xload(j).wait()

            @pl.when(below)
            def _():
                x_full.start()

                @pl.loop(0, 16)
                def _(j):
                    XT[pl.ds(128 * j, 128), pl.ds(512 * p, 512)] = Xo[j // 2, j % 2].T

            @pl.when(above)
            def _():
                g_core_in.wait_recv()

                @pl.loop(0, 8)
                def _(r):
                    XT[pl.ds(128 * r, 128), pl.ds(512 * p, 512)] = Xo[r, u].T

        @pl.when(above & (i >= 5) & (i % 2 == 1))
        def _():
            k = (i - 5) // 2
            layer_unit(k, 0)

            @pl.when(k == 0)
            def _():
                g_x_in.wait_recv()
                g_core2.start()
                x_half.start()
                g_cut_in.wait_recv()
                g_core3.start()
                g_core2_in.wait_recv()
                g_core3_in.wait_recv()

            @pl.when(k < 2)
            def _():
                layer_unit(k, 1)

        @pl.when(below & ((i == 9) | (i == 11)))
        def _():
            d_on((i - 9) // 2, 0)
            d_on((i - 9) // 2, 1)

    @pl.when(above)
    def _():
        @pl.loop(2, 4)
        def _(k):
            layer_unit(k, 1)

        rc(D.at[pl.ds(8 * c, 8), pl.ds(512 * (1 - p), 512)], Dp, O_X, pair).start()
        x_half_in.wait_recv()

        @pl.loop(0, 8)
        def _(r):
            XT[pl.ds(128 * r, 128), pl.ds(512 * (1 - p), 512)] = Xp[r, u].T

    LOW, HIGH, ALL = pl.ds(0, 128), pl.ds(128, 128), pl.ds(0, 256)

    def block(stage, m, h, e, rows):
        if stage == 1:
            return T.at[m, h, e, rows]
        return S.at[m, e, :, h, rows] if h == 0 else S.at[m, :, e, h, rows]

    def reduce(stage, i, m, h):
        e, to = axis(stage, h)
        rows = (LOW, HIGH, HIGH, LOW, LOW, HIGH)[i]
        src = block(stage, m, h, (e + (2, 2, 1, 3, 1, 3)[i]) % 4, rows)
        first, second = ((Ra, Rb), (Rc, Rd))[stage]
        if i < 2:
            dst = first.at[m, h, i]
        else:
            dst = second.at[m, h, i % 2, :, rows] if stage == 0 else second.at[m, h, i % 2, rows]
        return pltpu.make_async_remote_copy(
            src, dst, rs_s.at[stage, m, h, i], rs_r.at[stage, m, h, i],
            device_id=to((1, 3)[i % 2]), device_id_type=MESH)

    def reduce_start(stage, m, h):
        for i in range(4):
            reduce(stage, i, m, h).start()

    def reduce_on(stage, m):
        for h in range(2):
            e = axis(stage, h)[0]
            for i in range(2):
                reduce(stage, i, m, h).wait_recv()
                mine = block(stage, m, h, (e + (1, 3)[i]) % 4, (LOW, HIGH)[i])
                came = (Ra, Rc)[stage].at[m, h, i]
                if stage == 0:
                    @pl.loop(0, 4)
                    def _(b):
                        mine[b] = (mine[b].astype(F32) + came[b].astype(F32)).astype(BF)
                else:
                    mine[...] = (mine[...].astype(F32) + came[...].astype(F32)).astype(BF)
                reduce(stage, i + 4, m, h).start()

    def row_sums(m):
        for h in range(2):
            for i in range(2, 6):
                reduce(0, i, m, h).wait_recv()
            mine = block(0, m, h, axis(0, h)[0], ALL)

            @pl.loop(0, 4)
            def _(b):
                v = mine[b].astype(F32) + Rb[m, h, 0, b].astype(F32) + Rb[m, h, 1, b].astype(F32)
                T[m, h, b] = v.astype(BF)

                @pl.when(b == axis(1, h)[0])
                def _():
                    Tf[m, h] = v

            reduce_start(1, m, h)

    def finish(m):
        for h in range(2):
            for i in range(2, 6):
                reduce(1, i, m, h).wait_recv()
            v = Tf[m, h] + Rd[m, h, 0].astype(F32) + Rd[m, h, 1].astype(F32)
            F[h, 2 * m] = v[:128]
            F[h, 2 * m + 1] = v[128:]
            Nb[0, 0] = Nb[0, 0] + jnp.sum((v * v).reshape(32, 8, 128), axis=0)

    def input_part(n, t):
        for zz in range(4):
            left = jnp.concatenate([Gv[t, 8 + 2 * zz], Gv[t, 9 + 2 * zz]], axis=1)
            right = jnp.concatenate(
                [Wg[zz, yy, n // 4, pl.ds(256 * (n % 4), 256), :] for yy in range(4)], axis=1)
            part = dot_nt(left, right)
            acc[...] = part if zz == 0 else acc[...] + part
        lanes = pl.ds(128 * p, 128)
        mine = Gv[t, 8 + 4 * c + n // 2, :, pl.ds(pl.multiple_of(128 * (n % 2), 128), 128)]
        acc[:, lanes] = acc[:, lanes] + mine.astype(F32)

    def p_x(i):
        return rc(Gv.at[0, pl.ds(2 * i, 2)], Gv.at[1, pl.ds(2 * i, 2)], P_X + i, pair)

    def weight_grad(m):
        @pl.loop(0, 16)
        def _(q):
            v = dot_nn(XT[pl.ds(256 * m, 256), 0:512], Gv[0, q])
            v = v + dot_nn(XT[pl.ds(256 * m, 256), 512:1024], Gv[1, q])
            S[m, q // 4, q % 4, 0] = v[:, :128].astype(BF)
            S[m, q // 4, q % 4, 1] = v[:, 128:].astype(BF)

    def weight_grad_part(k):
        @pl.loop(0, 8)
        def _(i):
            cc, m = i // 4, i % 4
            right = jnp.concatenate([D[8 * cc + 2 * k], D[8 * cc + 2 * k + 1]], axis=1)
            v = [dot_nn(XT[pl.ds(1024 * h + 256 * m, 256), 0:1024], right) for h in range(2)]
            for rr in range(2):
                v0, v1 = (a[:, 128 * rr : 128 * rr + 128] for a in v)
                to = S.at[2 * (k // 2) + m // 2, 2 * cc + k % 2]
                to[2 * rr, m % 2] = low_lanes(v0, v1).astype(BF)
                to[2 * rr + 1, m % 2] = high_lanes(v0, v1).astype(BF)

    def natural(t):
        @pl.loop(0, 8)
        def _(a):
            b0, b1 = 8 * (a // 4) + a % 4, 8 * (a // 4) + 4 + a % 4
            v0 = D[b0, pl.ds(512 * t, 512)].astype(F32)
            v1 = D[b1, pl.ds(512 * t, 512)].astype(F32)
            Gv[t, 8 + a, :, 0:128] = low_lanes(v0, v1).astype(BF)
            Gv[t, 8 + a, :, 128:256] = high_lanes(v0, v1).astype(BF)

    def partner_part(i):
        @pl.loop(0, 2)
        def _(j):
            input_part(2 * i + j, 1 - p)
            Gv[0, 2 * i + j] = acc[...].astype(BF)

        p_x(i).start()

    def first_reduce(m):
        for h in range(2):
            reduce_start(0, m, h)

    @pl.when(below)
    def _():
        x_full.wait_recv()

        @pl.loop(0, 16)
        def _(i):
            XT[pl.ds(128 * i, 128), pl.ds(512 * (1 - p), 512)] = Xp[i // 2, i % 2].T

        @pl.loop(0, 2)
        def _(k):
            d_core_in(k, 0).wait_recv()
            d_core_in(k, 1).wait_recv()
            weight_grad_part(k)

        @pl.loop(0, 2)
        def _(m):
            first_reduce(m)

        g_cut.wait_send()

        @pl.loop(2, 4)
        def _(k):
            d_on(k, 0)

        @pl.loop(2, 4)
        def _(k):
            d_core_in(k, 0).wait_recv()

        natural(1 - p)

        @pl.loop(0, 2)
        def _(i):
            partner_part(2 * i)
            partner_part(2 * i + 1)
            reduce_on(0, i)

        @pl.loop(2, 4)
        def _(k):
            d_on(k, 1)

        @pl.loop(2, 4)
        def _(k):
            d_core_in(k, 1).wait_recv()
            weight_grad_part(k)

        @pl.loop(2, 4)
        def _(m):
            first_reduce(m)

        natural(p)

    Nb[0, 0] = jnp.zeros((8, 128), F32)

    @pl.loop(0, 8)
    def _(i):
        @pl.when(above & (i < 4))
        def _():
            weight_grad(i)
            first_reduce(i)

        @pl.when((i >= 1) & (i < 5) & (above | (i >= 3)))
        def _():
            reduce_on(0, i - 1)

        @pl.when((i >= 2) & (i < 6))
        def _():
            row_sums(i - 2)

        @pl.when((i >= 3) & (i < 7))
        def _():
            reduce_on(1, i - 3)

        @pl.when(i >= 4)
        def _():
            finish(i - 4)

    f_x = rc(F.at[1 - p], Fp, F_X, pair)

    @pl.when(above)
    def _():
        f_x.start()

    def own_part(i):
        @pl.when(below)
        def _():
            p_x(i).wait_recv()

            @pl.loop(0, 2)
            def _(j):
                n = 2 * i + j
                input_part(n, p)
                out_ref[:, pl.ds(pl.multiple_of(256 * n, 256), 256)] = (acc[...] + Gv[1, n].astype(F32)).astype(BF)

    steps = [near, [ydev(1), ydev(3), ydev(2)], [zdev(1), zdev(3), zdev(2)]]
    for i, targets in enumerate(steps):
        copies = [
            pltpu.make_async_remote_copy(
                Nb.at[i, 0], Nb.at[i, j + 1], ns.at[i, j], nr.at[i, j], device_id=to, device_id_type=MESH)
            for j, to in enumerate(targets)]
        for copy in copies:
            copy.start()
        own_part(i)
        for copy in copies:
            copy.wait_recv()
        v = Nb[i, 0]
        for j in range(len(targets)):
            v = v + Nb[i, j + 1]
        if i + 1 < len(steps):
            Nb[i + 1, 0] = v
        else:
            total = v
        for copy in copies:
            copy.wait_send()
    total = jnp.broadcast_to(jnp.sum(total, keepdims=True), (8, 128))
    clip = jnp.minimum(1.0, 1.0 / (jnp.sqrt(total / 33554432.0) + 1e-06))[0:1, :]

    @pl.when(above)
    def _():
        f_x.wait_recv()
        for r in range(8):
            grad_ref[pl.ds(256 * r + 128 * u, 128), :] = F[p, r] * clip
            grad_ref[pl.ds(256 * r + 128 * (1 - u), 128), :] = Fp[r] * clip

    @pl.when(below)
    def _():
        for r in range(8):
            m, half = r // 2, r % 2
            a, b = F[m % 2, 2 * (m // 2) + half], F[m % 2, 4 + 2 * (m // 2) + half]
            grad_ref[128 * r : 128 * r + 128, :] = low_lanes(a, b) * clip
            grad_ref[1024 + 128 * r : 1152 + 128 * r, :] = high_lanes(a, b) * clip

    own_part(3)

    @pl.when(above)
    def _():
        rc(Dp, Dp, O_X, pair).wait_recv()

        @pl.loop(0, 4)
        def _(a):
            for v0, v1, par in (
                (D[8 * c + a, pl.ds(512 * p, 512)], D[8 * c + 4 + a, pl.ds(512 * p, 512)], u),
                (Dp[a], Dp[4 + a], 1 - u),
            ):
                v0, v1 = v0.astype(F32), v1.astype(F32)
                out_ref[:, pl.ds(pl.multiple_of(512 * a + 128 * par, 128), 128)] = low_lanes(v0, v1).astype(BF)
                out_ref[:, pl.ds(pl.multiple_of(512 * a + 256 + 128 * par, 128), 128)] = high_lanes(v0, v1).astype(BF)

    @pl.loop(0, 8)
    def _(k):
        for h in range(2):
            for stage in range(2):
                for i in range(4):
                    gather(stage, i, k, h).wait_send()

    @pl.loop(0, 4)
    def _(k):
        for h in range(2):
            for stage in range(2):
                for i in range(6):
                    reduce(stage, i, k, h).wait_send()

    @pl.when(above)
    def _():
        for copy in (g_x, g_core, g_core2, g_core3, x_half, f_x):
            copy.wait_send()
        for k in range(8):
            w_x(k).wait_send()
        rc(Dp, Dp, O_X, pair).wait_send()

        @pl.loop(0, 4)
        def _(k):
            d_cut(k, 0).wait_send()
            d_cut(k, 1).wait_send()

    @pl.when(below)
    def _():
        x_full.wait_send()

        @pl.loop(0, 4)
        def _(k):
            d_core(k, 0).wait_send()
            d_core(k, 1).wait_send()
            p_x(k).wait_send()


def per_device(saved_input, out_grad, master_weight, moment1, moment2):
    vmem = pl.BlockSpec(memory_space=pltpu.VMEM)
    hbm = pl.BlockSpec(memory_space=pl.ANY)
    dma = pltpu.SemaphoreType.DMA
    input_grad, clipped = pl.pallas_call(
        kernel,
        out_shape=(
            jax.ShapeDtypeStruct((512, 2048), BF),
            jax.ShapeDtypeStruct((2048, 128), F32),
        ),
        in_specs=[hbm, hbm, vmem],
        out_specs=(vmem, vmem),
        scratch_shapes=[
            pltpu.VMEM((4, 4, 2, 1024, 128), BF),
            pltpu.VMEM((1024, 128), BF),
            pltpu.VMEM((2, 16, 512, 256), BF),
            pltpu.VMEM((16, 1024, 128), BF),
            pltpu.VMEM((8, 512, 128), BF),
            pltpu.VMEM((8, 2, 512, 128), BF),
            pltpu.VMEM((8, 2, 512, 128), BF),
            pltpu.VMEM((2048, 1024), BF),
            pltpu.VMEM((4, 4, 4, 2, 256, 128), BF),
            pltpu.VMEM((4, 2, 2, 4, 128, 128), BF),
            pltpu.VMEM((4, 2, 2, 4, 256, 128), BF),
            pltpu.VMEM((4, 2, 2, 128, 128), BF),
            pltpu.VMEM((4, 2, 2, 256, 128), BF),
            pltpu.VMEM((4, 2, 4, 256, 128), BF),
            pltpu.VMEM((4, 2, 256, 128), F32),
            pltpu.VMEM((2, 8, 128, 128), F32),
            pltpu.VMEM((8, 128, 128), F32),
            pltpu.VMEM((512, 256), F32),
            pltpu.VMEM((3, 8, 8, 128), F32),
            dma((16,)), dma((8,)),
            dma((2, 8, 2, 4)), dma((2, 8, 2, 4)),
            dma((2, 4, 2, 6)), dma((2, 4, 2, 6)),
            dma((36,)), dma((36,)),
            dma((3, 7)), dma((3, 7)),
        ],
        compiler_params=pltpu.CompilerParams(
            collective_id=0, has_side_effects=True, vmem_limit_bytes=62 * 2**20),
    )(saved_input.reshape(512, 2048), out_grad.reshape(512, 2048), master_weight[0])
    master = master_weight[0]
    new_moment1 = 0.9 * moment1[0] + 0.1 * clipped
    new_moment2 = 0.95 * moment2[0] + 0.05 * clipped * clipped
    first_fix = 1.0 - 0.9**10
    second_fix = 1.0 - 0.95**10
    update = new_moment1 / first_fix / (jnp.sqrt(new_moment2 / second_fix) + 1e-08)
    new_weight = master - 0.01 * (update + 0.1 * master)
    return (input_grad.reshape(1, 2, 256, 2048), new_weight[None], new_moment1[None], new_moment2[None])


def solution(mesh):
    return jax.shard_map(
        per_device,
        mesh=mesh,
        in_specs=(
            P("section", None, "dp", "mp"),
            P(None, "dp", "mp"),
            P("section", "mp", "dp"),
            P("section", "mp", "dp"),
            P("section", "mp", "dp"),
        ),
        out_specs=(
            P("section", None, "dp", "mp"),
            P("section", "mp", "dp"),
            P("section", "mp", "dp"),
            P("section", "mp", "dp"),
        ),
        check_vma=False,
    )
```

```python
import jax
import jax.numpy as jnp
from jax import lax
from jax.experimental import pallas as pl
from jax.experimental.pallas import tpu as pltpu
from jax.sharding import PartitionSpec as P

MESH = pl.DeviceIdType.MESH
BF = jnp.bfloat16
F32 = jnp.float32
X_X, G_X, G_CUT, G_CORE, G_CORE2, G_CORE3, D_CUT, D_CORE, P_X, O_X, F_X, W_X = 0, 1, 2, 3, 4, 5, 6, 14, 22, 26, 27, 31


def dot_nt(a, b):
    return lax.dot_general(a, b, (((1,), (1,)), ((), ())), preferred_element_type=F32)


def dot_nn(a, b):
    return jnp.dot(a, b, preferred_element_type=F32)


def lane_group(x):
    return lax.broadcasted_iota(jnp.int32, x.shape, 1) // 32


def merge(parts, take):
    out = None
    for a, part in enumerate(parts):
        moved = pltpu.roll(part, (32 * (a - take(a))) % 128, 1)
        out = moved if out is None else jnp.where(lane_group(part) == a, moved, out)
    return out


def transpose(parts):
    g = lane_group(parts[0])
    even, odd = g % 2 == 0, g < 2
    a, b, c, d = parts
    a, b = jnp.where(even, a, pltpu.roll(b, 32, 1)), jnp.where(even, pltpu.roll(a, 96, 1), b)
    c, d = jnp.where(even, c, pltpu.roll(d, 32, 1)), jnp.where(even, pltpu.roll(c, 96, 1), d)
    a, c = jnp.where(odd, a, pltpu.roll(c, 64, 1)), jnp.where(odd, pltpu.roll(a, 64, 1), c)
    b, d = jnp.where(odd, b, pltpu.roll(d, 64, 1)), jnp.where(odd, pltpu.roll(b, 64, 1), d)
    return a, b, c, d


def kernel(
    x_hbm, g_hbm, w_ref, out_ref, grad_ref,
    Wg, Wx, Gv, D, Dp, Xo, Xp, XT, S, Ra, Rb, Rc, Rd, T, Tf, F, Fp, acc, Own, Nb,
    ldx, ldg, ag_s, ag_r, rs_s, rs_r, ms, mr, ns, nr,
):
    s = lax.axis_index("section")
    d = lax.axis_index("dp")
    c = lax.axis_index("mp")
    z, y, p = d // 8, (d // 2) % 4, d % 2
    u = jnp.where(s == 1, 1 - p, p)

    def dev(s_, z_, y_, p_, c_):
        return (s_, (z_ * 4 + y_) * 2 + p_, c_)

    def zdev(o):
        return dev(s, (z + o) % 4, y, p, c)

    def ydev(o):
        return dev(s, z, (y + o) % 4, p, c)

    pair = dev(s, z, y, 1 - p, c)
    cut = dev(1 - s, z, y, 1 - p, c)
    core = dev(s, z, y, p, 1 - c)
    near = [core, pair, cut, dev(s, z, y, 1 - p, 1 - c), dev(1 - s, z, y, 1 - p, 1 - c),
            dev(1 - s, z, y, p, c), dev(1 - s, z, y, p, 1 - c)]
    above = s == 1
    below = s == 0

    def rc(src, dst, i, to):
        return pltpu.make_async_remote_copy(src, dst, ms.at[i], mr.at[i], device_id=to, device_id_type=MESH)

    def xload(i):
        return pltpu.make_async_copy(x_hbm.at[:, pl.ds(128 * i, 128)], Xo.at[i // 2, i % 2], ldx.at[i])

    def gload(i, dst):
        return pltpu.make_async_copy(g_hbm.at[:, pl.ds(256 * i, 256)], dst, ldg.at[i])

    for i in range(16):
        xload(i).start()

    @pl.when(above)
    def _():
        for i in range(8):
            gload(i, Gv.at[p, 8 * c + i]).start()

    @pl.when(below)
    def _():
        for i in range(4, 8):
            gload(i, Gv.at[0, 8 + i]).start()

    barrier = pltpu.get_barrier_semaphore()
    peers = [zdev(1), zdev(2), zdev(3), ydev(1), ydev(2), ydev(3), *near]
    for to in peers:
        pl.semaphore_signal(barrier, inc=1, device_id=to, device_id_type=MESH)

    @pl.when(above)
    def _():
        for a in range(32):
            rows = 256 * (a % 8) + 32 * (a // 8)
            Wg[z, y, p, 32 * a : 32 * a + 32] = w_ref[pl.ds(rows + 128 * u, 32), :].astype(BF)
            Wx[32 * a : 32 * a + 32] = w_ref[pl.ds(rows + 128 * (1 - u), 32), :].astype(BF)

    @pl.when(below)
    def _():
        for r in range(8):
            Wg[z, y, r // 4, 256 * (r % 4) : 256 * (r % 4) + 256] = w_ref[256 * r : 256 * r + 256, :].astype(BF)

    pl.semaphore_wait(barrier, len(peers))

    def w_x(k):
        rows = pl.ds(128 * k, 128)
        return rc(Wx.at[rows], Wg.at[z, y, p, rows], W_X + k, pair)

    g_x = rc(Gv.at[p, pl.ds(8 * c, 4)], Gv.at[p, pl.ds(8 * c, 4)], G_X, pair)
    g_x_in = rc(Gv.at[1 - p, pl.ds(8 * c, 4)], Gv.at[1 - p, pl.ds(8 * c, 4)], G_X, pair)
    g_cut = rc(Gv.at[0, pl.ds(12, 4)], Gv.at[p, pl.ds(8 * c + 4, 4)], G_CUT, cut)
    g_cut_in = rc(Gv.at[1 - p, pl.ds(8 * c + 4, 4)], Gv.at[1 - p, pl.ds(8 * c + 4, 4)], G_CUT, cut)
    g_core = rc(Gv.at[p, pl.ds(8 * c, 8)], Gv.at[p, pl.ds(8 * c, 8)], G_CORE, core)
    g_core_in = rc(Gv.at[p, pl.ds(8 * (1 - c), 8)], Gv.at[p, pl.ds(8 * (1 - c), 8)], G_CORE, core)
    g_core2 = rc(Gv.at[1 - p, pl.ds(8 * c, 4)], Gv.at[1 - p, pl.ds(8 * c, 4)], G_CORE2, core)
    g_core2_in = rc(Gv.at[1 - p, pl.ds(8 * (1 - c), 4)], Gv.at[1 - p, pl.ds(8 * (1 - c), 4)], G_CORE2, core)
    g_core3 = rc(Gv.at[1 - p, pl.ds(8 * c + 4, 4)], Gv.at[1 - p, pl.ds(8 * c + 4, 4)], G_CORE3, core)
    g_core3_in = rc(Gv.at[1 - p, pl.ds(8 * (1 - c) + 4, 4)], Gv.at[1 - p, pl.ds(8 * (1 - c) + 4, 4)], G_CORE3, core)
    x_half = rc(Xo.at[:, 1 - u], Xp.at[:, 1 - u], X_X, pair)
    x_half_in = rc(Xo.at[:, u], Xp.at[:, u], X_X, pair)
    x_full = rc(Xo, Xp, X_X, pair)

    def axis(stage, h):
        return (z, zdev) if stage == h else (y, ydev)

    def gather(stage, i, k, h):
        e, to = axis(stage, h)
        e = (e, e, (e + 3) % 4, (e + 1) % 4)[i]
        rows = pl.ds(128 * k + (0, 0, 0, 64)[i], (128, 128, 64, 64)[i])
        if stage == 0:
            ref = Wg.at[e, y, h, rows] if h == 0 else Wg.at[z, e, h, rows]
        else:
            ref = Wg.at[:, e, h, rows] if h == 0 else Wg.at[e, :, h, rows]
        return pltpu.make_async_remote_copy(
            ref, ref, ag_s.at[stage, k, h, i], ag_r.at[stage, k, h, i],
            device_id=to((1, 3, 1, 3)[i]), device_id_type=MESH)

    def gather_on(stage, k):
        for h in range(2):
            for i in range(2):
                gather(stage, i, k, h).wait_recv()
                gather(stage, i + 2, k, h).start()

    def gather_end(stage, k):
        for h in range(2):
            for i in (2, 3):
                gather(stage, i, k, h).wait_recv()

    @pl.when(above)
    def _():
        for k in range(8):
            w_x(k).start()
        for i in range(8):
            gload(i, Gv.at[p, 8 * c + i]).wait()
        g_x.start()
        g_core.start()

    @pl.when(below)
    def _():
        for i in range(4, 8):
            gload(i, Gv.at[0, 8 + i]).wait()
        g_cut.start()

    def gather_begin(k):
        @pl.when(above)
        def _():
            w_x(k).wait_recv()

        for h in range(2):
            for i in range(2):
                gather(0, i, k, h).start()

    def gather_rows(k):
        for h in range(2):
            for i in range(2):
                gather(1, i, k, h).start()

    def unit(k, j):
        t = jnp.where(s == 1, p, 1 - p) if j == 0 else jnp.where(s == 1, 1 - p, p)
        return t, D.at[pl.ds(8 * c + 2 * k, 2), pl.ds(512 * t, 512)]

    def from_core(k, j):
        t = unit(k, j)[0]
        return D.at[pl.ds(8 * (1 - c) + 2 * k, 2), pl.ds(512 * t, 512)]

    def d_cut(k, j):
        ref = unit(k, j)[1]
        return rc(ref, ref, D_CUT + 2 * k + j, cut)

    def d_core(k, j):
        ref = unit(k, j)[1]
        return rc(ref, ref, D_CORE + 2 * k + j, core)

    def d_core_in(k, j):
        ref = from_core(k, j)
        return rc(ref, ref, D_CORE + 2 * k + j, core)

    def d_on(k, j):
        d_cut(k, j).wait_recv()
        d_core(k, j).start()

    def layer_unit(k, j):
        t = unit(k, j)[0]
        for zz in range(4):
            left = jnp.concatenate([Gv[t, 4 * zz + yy] for yy in range(4)], axis=1)
            right = jnp.concatenate(
                [Wg[zz, yy, h, pl.ds(256 * k, 256), :] for yy in range(4) for h in range(2)], axis=1)
            part = dot_nt(left, right)
            acc[...] = part if zz == 0 else acc[...] + part
        for rr in range(2):
            mine = [Gv[t, 8 * c + 4 * rr + a, :, pl.ds(128 * u, 128)].astype(F32) for a in range(4)]
            mine = merge(mine, lambda a: k)
            D[8 * c + 2 * k + rr, pl.ds(512 * t, 512)] = (acc[:, 128 * rr : 128 * rr + 128] + mine).astype(BF)
        d_cut(k, j).start()

    LOW, HIGH, ALL = pl.ds(0, 128), pl.ds(128, 128), pl.ds(0, 256)

    def block(stage, m, h, e, rows):
        if stage == 1:
            return T.at[m, h, e, rows]
        return S.at[m, e, :, h, rows] if h == 0 else S.at[m, :, e, h, rows]

    def reduce(stage, i, m, h):
        e, to = axis(stage, h)
        rows = (LOW, HIGH, HIGH, LOW, LOW, HIGH)[i]
        src = block(stage, m, h, (e + (2, 2, 1, 3, 1, 3)[i]) % 4, rows)
        first, second = ((Ra, Rb), (Rc, Rd))[stage]
        if i < 2:
            dst = first.at[m, h, i]
        else:
            dst = second.at[m, h, i % 2, :, rows] if stage == 0 else second.at[m, h, i % 2, rows]
        return pltpu.make_async_remote_copy(
            src, dst, rs_s.at[stage, m, h, i], rs_r.at[stage, m, h, i],
            device_id=to((1, 3)[i % 2]), device_id_type=MESH)

    def reduce_start(stage, m, h):
        for i in range(4):
            reduce(stage, i, m, h).start()

    def reduce_on(stage, m):
        for h in range(2):
            e = axis(stage, h)[0]
            for i in range(2):
                reduce(stage, i, m, h).wait_recv()
                mine = block(stage, m, h, (e + (1, 3)[i]) % 4, (LOW, HIGH)[i])
                came = (Ra, Rc)[stage].at[m, h, i]
                if stage == 0:
                    @pl.loop(0, 4)
                    def _(b):
                        mine[b] = (mine[b].astype(F32) + came[b].astype(F32)).astype(BF)
                else:
                    mine[...] = (mine[...].astype(F32) + came[...].astype(F32)).astype(BF)
                reduce(stage, i + 4, m, h).start()

    def row_sums(m):
        for h in range(2):
            for i in range(2, 6):
                reduce(0, i, m, h).wait_recv()
            mine = block(0, m, h, axis(0, h)[0], ALL)

            @pl.loop(0, 4)
            def _(b):
                v = mine[b].astype(F32) + Rb[m, h, 0, b].astype(F32) + Rb[m, h, 1, b].astype(F32)
                T[m, h, b] = v.astype(BF)

                @pl.when(b == axis(1, h)[0])
                def _():
                    Tf[m, h] = v

            reduce_start(1, m, h)

    def f_x(m):
        rows = pl.ds(2 * m, 2)
        return rc(F.at[1 - p, rows], Fp.at[rows], F_X + m, pair)

    def finish(m):
        for h in range(2):
            for i in range(2, 6):
                reduce(1, i, m, h).wait_recv()
            v = Tf[m, h] + Rd[m, h, 0].astype(F32) + Rd[m, h, 1].astype(F32)
            F[h, 2 * m] = v[:128]
            F[h, 2 * m + 1] = v[128:]
            Nb[0, 0] = Nb[0, 0] + jnp.sum((v * v).reshape(32, 8, 128), axis=0)

        @pl.when(above)
        def _():
            f_x(m).start()

    def input_part(n, t, to):
        for zz in range(4):
            left = jnp.concatenate([Gv[t, 8 + 2 * zz], Gv[t, 9 + 2 * zz]], axis=1)
            right = jnp.concatenate(
                [Wg[zz, yy, n // 4, pl.ds(256 * (n % 4), 256), :] for yy in range(4)], axis=1)
            part = dot_nt(left, right)
            to[...] = part if zz == 0 else to[...] + part
        lanes = pl.ds(128 * p, 128)
        mine = Gv[t, 8 + 4 * c + n // 2, :, pl.ds(pl.multiple_of(128 * (n % 2), 128), 128)]
        to[:, lanes] = to[:, lanes] + mine.astype(F32)

    def p_x(i):
        return rc(Gv.at[0, pl.ds(2 * i, 2)], Gv.at[1, pl.ds(2 * i, 2)], P_X + i, pair)

    def weight_grad(m):
        @pl.loop(0, 16)
        def _(q):
            v = dot_nn(XT[pl.ds(256 * m, 256), 0:512], Gv[0, q])
            v = v + dot_nn(XT[pl.ds(256 * m, 256), 512:1024], Gv[1, q])
            S[m, q // 4, q % 4, 0] = v[:, :128].astype(BF)
            S[m, q // 4, q % 4, 1] = v[:, 128:].astype(BF)

    def weight_grad_part(k):
        @pl.loop(0, 4)
        def _(i):
            cc, half = i // 2, i % 2
            right = jnp.concatenate([D[8 * cc + 2 * k], D[8 * cc + 2 * k + 1]], axis=1)
            v = [dot_nn(XT[pl.ds(512 * g + 256 * half, 256), 0:1024], right) for g in range(4)]
            for rr in range(2):
                for a, b in enumerate(transpose([x[:, 128 * rr : 128 * rr + 128] for x in v])):
                    S[k, 2 * cc + rr, a, half] = b.astype(BF)

    def weight_grad_from(k):
        @pl.when(k < 2)
        def _():
            d_core_in(k, 0).wait_recv()

        d_core_in(k, 1).wait_recv()
        weight_grad_part(k)
        first_reduce(k)

    def natural(t):
        @pl.loop(0, 4)
        def _(i):
            b = 8 * (i // 2) + i % 2
            v = transpose([D[b + 2 * g, pl.ds(512 * t, 512)].astype(F32) for g in range(4)])
            for a in range(4):
                Gv[t, 8 + 2 * i + a // 2, :, 128 * (a % 2) : 128 * (a % 2) + 128] = v[a].astype(BF)

    def partner_part(i):
        @pl.loop(0, 2)
        def _(j):
            input_part(2 * i + j, 1 - p, acc)
            Gv[0, 2 * i + j] = acc[...].astype(BF)

    def first_reduce(m):
        for h in range(2):
            reduce_start(0, m, h)

    gather_begin(0)
    gather_begin(1)

    @pl.loop(0, 12)
    def _(i):
        @pl.when(i < 6)
        def _():
            gather_begin(i + 2)

        @pl.when(i < 8)
        def _():
            gather_on(0, i)

        @pl.when((i >= 1) & (i < 9))
        def _():
            gather_end(0, i - 1)
            gather_rows(i - 1)

        @pl.when((i >= 3) & (i < 11))
        def _():
            gather_on(1, i - 3)

        @pl.when(i >= 4)
        def _():
            gather_end(1, i - 4)

        @pl.when(i == 4)
        def _():
            for j in range(16):
                xload(j).wait()

            @pl.when(below)
            def _():
                x_full.start()

                @pl.loop(0, 16)
                def _(j):
                    XT[pl.ds(128 * j, 128), pl.ds(512 * p, 512)] = Xo[j // 2, j % 2].T

            @pl.when(above)
            def _():
                g_core_in.wait_recv()

                @pl.loop(0, 8)
                def _(r):
                    XT[pl.ds(128 * r, 128), pl.ds(512 * p, 512)] = Xo[r, u].T

        @pl.when(above & (i >= 5) & (i % 2 == 1))
        def _():
            k = (i - 5) // 2
            layer_unit(k, 0)

            @pl.when(k == 0)
            def _():
                g_x_in.wait_recv()
                g_core2.start()
                x_half.start()
                g_cut_in.wait_recv()
                g_core3.start()
                g_core2_in.wait_recv()
                g_core3_in.wait_recv()

            @pl.when(k < 2)
            def _():
                layer_unit(k, 1)

        @pl.when(above & (i == 10))
        def _():
            x_half_in.wait_recv()

            @pl.loop(0, 8)
            def _(r):
                XT[pl.ds(128 * r, 128), pl.ds(512 * (1 - p), 512)] = Xp[r, u].T

            weight_grad(0)
            first_reduce(0)

        @pl.when(below & ((i == 9) | (i == 11)))
        def _():
            d_on((i - 9) // 2, 0)
            d_on((i - 9) // 2, 1)

        @pl.when(below & (i == 10))
        def _():
            x_full.wait_recv()

            @pl.loop(0, 16)
            def _(j):
                XT[pl.ds(128 * j, 128), pl.ds(512 * (1 - p), 512)] = Xp[j // 2, j % 2].T

        @pl.when(below & (i >= 10))
        def _():
            weight_grad_from(i - 10)

    @pl.when(above)
    def _():
        @pl.loop(2, 4)
        def _(k):
            layer_unit(k, 1)

        rc(D.at[pl.ds(8 * c, 8), pl.ds(512 * (1 - p), 512)], Dp, O_X, pair).start()
    @pl.when(below)
    def _():
        g_cut.wait_send()

        @pl.loop(2, 4)
        def _(k):
            d_on(k, 0)

        @pl.loop(2, 4)
        def _(k):
            d_core_in(k, 0).wait_recv()

        natural(1 - p)

        partner_part(0)
        p_x(0).start()

        @pl.loop(2, 4)
        def _(k):
            d_on(k, 1)
            weight_grad_from(k)
            partner_part(k - 1)
            p_x(k - 1).start()

        partner_part(3)
        p_x(3).start()
        reduce_on(0, 0)
        reduce_on(0, 1)

        natural(p)

    Nb[0, 0] = jnp.zeros((8, 128), F32)

    @pl.loop(0, 8)
    def _(i):
        @pl.when(above & (i >= 1) & (i < 4))
        def _():
            weight_grad(i)
            first_reduce(i)

        @pl.when((i >= 1) & (i < 5) & (above | (i >= 3)))
        def _():
            reduce_on(0, i - 1)

        @pl.when((i >= 2) & (i < 6))
        def _():
            row_sums(i - 2)

        @pl.when((i >= 3) & (i < 7))
        def _():
            reduce_on(1, i - 3)

        @pl.when(i >= 4)
        def _():
            finish(i - 4)

        @pl.when(below & (i >= 2) & (i < 6))
        def _():
            for j in range(2):
                input_part(2 * (i - 2) + j, p, Own.at[2 * (i - 2) + j])

    def own_part(i):
        @pl.when(below)
        def _():
            p_x(i).wait_recv()
            for n in (2 * i, 2 * i + 1):
                out_ref[:, 256 * n : 256 * n + 256] = (Own[n] + Gv[1, n].astype(F32)).astype(BF)

    steps = [near, [ydev(1), ydev(3), ydev(2)], [zdev(1), zdev(3), zdev(2)]]
    for i, targets in enumerate(steps):
        copies = [
            pltpu.make_async_remote_copy(
                Nb.at[i, 0], Nb.at[i, j + 1], ns.at[i, j], nr.at[i, j], device_id=to, device_id_type=MESH)
            for j, to in enumerate(targets)]
        for copy in copies:
            copy.start()
        for copy in copies:
            copy.wait_recv()
        v = Nb[i, 0]
        for j in range(len(targets)):
            v = v + Nb[i, j + 1]
        if i + 1 < len(steps):
            Nb[i + 1, 0] = v
        else:
            total = v
        for copy in copies:
            copy.wait_send()
    total = jnp.broadcast_to(jnp.sum(total, keepdims=True), (8, 128))
    clip = jnp.minimum(1.0, 1.0 / (jnp.sqrt(total / 33554432.0) + 1e-06))[0:1, :]

    @pl.when(above)
    def _():
        for m in range(4):
            f_x(m).wait_recv()
        for r in range(8):
            grad_ref[pl.ds(256 * r + 128 * u, 128), :] = F[p, r] * clip
            grad_ref[pl.ds(256 * r + 128 * (1 - u), 128), :] = Fp[r] * clip

    @pl.when(below)
    def _():
        for r in range(4):
            half, low = r // 2, r % 2
            v = transpose([F[half, 2 * k + low] for k in range(4)])
            for g in range(4):
                rows = 512 * g + 256 * half + 128 * low
                grad_ref[rows : rows + 128, :] = v[g] * clip

    for i in range(4):
        own_part(i)

    @pl.when(above)
    def _():
        rc(Dp, Dp, O_X, pair).wait_recv()

        @pl.loop(0, 2)
        def _(i):
            for par, src in ((u, D.at[pl.ds(8 * c, 8), pl.ds(512 * p, 512)]), (1 - u, Dp)):
                v = transpose([src[2 * g + i].astype(F32) for g in range(4)])
                for a in range(4):
                    lanes = pl.ds(pl.multiple_of(1024 * i + 256 * a + 128 * par, 128), 128)
                    out_ref[:, lanes] = v[a].astype(BF)

    @pl.loop(0, 8)
    def _(k):
        for h in range(2):
            for stage in range(2):
                for i in range(4):
                    gather(stage, i, k, h).wait_send()

    @pl.loop(0, 4)
    def _(k):
        for h in range(2):
            for stage in range(2):
                for i in range(6):
                    reduce(stage, i, k, h).wait_send()

    @pl.when(above)
    def _():
        for copy in (g_x, g_core, g_core2, g_core3, x_half):
            copy.wait_send()
        for m in range(4):
            f_x(m).wait_send()
        for k in range(8):
            w_x(k).wait_send()
        rc(Dp, Dp, O_X, pair).wait_send()

        @pl.loop(0, 4)
        def _(k):
            d_cut(k, 0).wait_send()
            d_cut(k, 1).wait_send()

    @pl.when(below)
    def _():
        x_full.wait_send()

        @pl.loop(0, 4)
        def _(k):
            d_core(k, 0).wait_send()
            d_core(k, 1).wait_send()

        for i in range(4):
            p_x(i).wait_send()


def per_device(saved_input, out_grad, master_weight, moment1, moment2):
    vmem = pl.BlockSpec(memory_space=pltpu.VMEM)
    hbm = pl.BlockSpec(memory_space=pl.ANY)
    dma = pltpu.SemaphoreType.DMA
    input_grad, clipped = pl.pallas_call(
        kernel,
        out_shape=(
            jax.ShapeDtypeStruct((512, 2048), BF),
            jax.ShapeDtypeStruct((2048, 128), F32),
        ),
        in_specs=[hbm, hbm, vmem],
        out_specs=(vmem, vmem),
        scratch_shapes=[
            pltpu.VMEM((4, 4, 2, 1024, 128), BF),
            pltpu.VMEM((1024, 128), BF),
            pltpu.VMEM((2, 16, 512, 256), BF),
            pltpu.VMEM((16, 1024, 128), BF),
            pltpu.VMEM((8, 512, 128), BF),
            pltpu.VMEM((8, 2, 512, 128), BF),
            pltpu.VMEM((8, 2, 512, 128), BF),
            pltpu.VMEM((2048, 1024), BF),
            pltpu.VMEM((4, 4, 4, 2, 256, 128), BF),
            pltpu.VMEM((4, 2, 2, 4, 128, 128), BF),
            pltpu.VMEM((4, 2, 2, 4, 256, 128), BF),
            pltpu.VMEM((4, 2, 2, 128, 128), BF),
            pltpu.VMEM((4, 2, 2, 256, 128), BF),
            pltpu.VMEM((4, 2, 4, 256, 128), BF),
            pltpu.VMEM((4, 2, 256, 128), F32),
            pltpu.VMEM((2, 8, 128, 128), F32),
            pltpu.VMEM((8, 128, 128), F32),
            pltpu.VMEM((512, 256), F32),
            pltpu.VMEM((8, 512, 256), F32),
            pltpu.VMEM((3, 8, 8, 128), F32),
            dma((16,)), dma((8,)),
            dma((2, 8, 2, 4)), dma((2, 8, 2, 4)),
            dma((2, 4, 2, 6)), dma((2, 4, 2, 6)),
            dma((39,)), dma((39,)),
            dma((3, 7)), dma((3, 7)),
        ],
        compiler_params=pltpu.CompilerParams(
            collective_id=0, has_side_effects=True, vmem_limit_bytes=62 * 2**20),
    )(saved_input.reshape(512, 2048), out_grad.reshape(512, 2048), master_weight[0])
    master = master_weight[0]
    new_moment1 = 0.9 * moment1[0] + 0.1 * clipped
    new_moment2 = 0.95 * moment2[0] + 0.05 * clipped * clipped
    first_fix = 1.0 - 0.9**10
    second_fix = 1.0 - 0.95**10
    update = new_moment1 / first_fix / (jnp.sqrt(new_moment2 / second_fix) + 1e-08)
    new_weight = master - 0.01 * (update + 0.1 * master)
    return (input_grad.reshape(1, 2, 256, 2048), new_weight[None], new_moment1[None], new_moment2[None])


def solution(mesh):
    return jax.shard_map(
        per_device,
        mesh=mesh,
        in_specs=(
            P("section", None, "dp", "mp"),
            P(None, "dp", "mp"),
            P("section", "mp", "dp"),
            P("section", "mp", "dp"),
            P("section", "mp", "dp"),
        ),
        out_specs=(
            P("section", None, "dp", "mp"),
            P("section", "mp", "dp"),
            P("section", "mp", "dp"),
            P("section", "mp", "dp"),
        ),
        check_vma=False,
    )
```

```python
import jax
import jax.numpy as jnp
from jax import lax
from jax.experimental import pallas as pl
from jax.experimental.pallas import tpu as pltpu
from jax.sharding import PartitionSpec as P

MESH = pl.DeviceIdType.MESH
BF = jnp.bfloat16
F32 = jnp.float32
X_X, G_X, G_CUT, G_CORE, G_CORE2, G_CORE3, D_CUT, D_CORE, P_X, O_X, F_X, W_X = 0, 1, 2, 3, 4, 5, 6, 14, 22, 26, 27, 31


def dot_nt(a, b):
    return lax.dot_general(a, b, (((1,), (1,)), ((), ())), preferred_element_type=F32)


def dot_nn(a, b):
    return jnp.dot(a, b, preferred_element_type=F32)


def lane_group(x):
    return lax.broadcasted_iota(jnp.int32, x.shape, 1) // 32


def merge(parts, take):
    out = None
    for a, part in enumerate(parts):
        moved = pltpu.roll(part, (32 * (a - take(a))) % 128, 1)
        out = moved if out is None else jnp.where(lane_group(part) == a, moved, out)
    return out


def transpose(parts):
    g = lane_group(parts[0])
    even, odd = g % 2 == 0, g < 2
    a, b, c, d = parts
    a, b = jnp.where(even, a, pltpu.roll(b, 32, 1)), jnp.where(even, pltpu.roll(a, 96, 1), b)
    c, d = jnp.where(even, c, pltpu.roll(d, 32, 1)), jnp.where(even, pltpu.roll(c, 96, 1), d)
    a, c = jnp.where(odd, a, pltpu.roll(c, 64, 1)), jnp.where(odd, pltpu.roll(a, 64, 1), c)
    b, d = jnp.where(odd, b, pltpu.roll(d, 64, 1)), jnp.where(odd, pltpu.roll(b, 64, 1), d)
    return a, b, c, d


def kernel(
    x_hbm, g_hbm, w_ref, out_ref, grad_ref,
    Wg, Wx, Gv, D, Dp, Xo, Xp, XT, S, Ra, Rb, Rc, Rd, T, Tf, F, Fp, acc, Own, Nb,
    ldx, ldg, ag_s, ag_r, rs_s, rs_r, ms, mr, ns, nr,
):
    s = lax.axis_index("section")
    d = lax.axis_index("dp")
    c = lax.axis_index("mp")
    z, y, p = d // 8, (d // 2) % 4, d % 2
    u = jnp.where(s == 1, 1 - p, p)

    def dev(s_, z_, y_, p_, c_):
        return (s_, (z_ * 4 + y_) * 2 + p_, c_)

    def zdev(o):
        return dev(s, (z + o) % 4, y, p, c)

    def ydev(o):
        return dev(s, z, (y + o) % 4, p, c)

    pair = dev(s, z, y, 1 - p, c)
    cut = dev(1 - s, z, y, 1 - p, c)
    core = dev(s, z, y, p, 1 - c)
    near = [core, pair, cut, dev(s, z, y, 1 - p, 1 - c), dev(1 - s, z, y, 1 - p, 1 - c),
            dev(1 - s, z, y, p, c), dev(1 - s, z, y, p, 1 - c)]
    above = s == 1
    below = s == 0

    def rc(src, dst, i, to):
        return pltpu.make_async_remote_copy(src, dst, ms.at[i], mr.at[i], device_id=to, device_id_type=MESH)

    def xload(i):
        return pltpu.make_async_copy(x_hbm.at[:, pl.ds(128 * i, 128)], Xo.at[i // 2, i % 2], ldx.at[i])

    def gload(i, dst):
        return pltpu.make_async_copy(g_hbm.at[:, pl.ds(256 * i, 256)], dst, ldg.at[i])

    @pl.when(above)
    def _():
        for i in range(8):
            gload(i, Gv.at[p, 8 * c + i]).start()

    @pl.when(below)
    def _():
        for i in range(4, 8):
            gload(i, Gv.at[0, 8 + i]).start()

    for i in range(16):
        xload(i).start()

    barrier = pltpu.get_barrier_semaphore()
    peers = [zdev(1), zdev(2), zdev(3), ydev(1), ydev(2), ydev(3), *near]
    for to in peers:
        pl.semaphore_signal(barrier, inc=1, device_id=to, device_id_type=MESH)

    @pl.when(above)
    def _():
        for a in range(32):
            rows = 256 * (a % 8) + 32 * (a // 8)
            Wg[z, y, p, 32 * a : 32 * a + 32] = w_ref[pl.ds(rows + 128 * u, 32), :].astype(BF)
            Wx[32 * a : 32 * a + 32] = w_ref[pl.ds(rows + 128 * (1 - u), 32), :].astype(BF)

    @pl.when(below)
    def _():
        for r in range(8):
            Wg[z, y, r // 4, 256 * (r % 4) : 256 * (r % 4) + 256] = w_ref[256 * r : 256 * r + 256, :].astype(BF)

    pl.semaphore_wait(barrier, len(peers))

    def w_x(k):
        rows = pl.ds(128 * k, 128)
        return rc(Wx.at[rows], Wg.at[z, y, p, rows], W_X + k, pair)

    g_x = rc(Gv.at[p, pl.ds(8 * c, 4)], Gv.at[p, pl.ds(8 * c, 4)], G_X, pair)
    g_x_in = rc(Gv.at[1 - p, pl.ds(8 * c, 4)], Gv.at[1 - p, pl.ds(8 * c, 4)], G_X, pair)
    g_cut = rc(Gv.at[0, pl.ds(12, 4)], Gv.at[p, pl.ds(8 * c + 4, 4)], G_CUT, cut)
    g_cut_in = rc(Gv.at[1 - p, pl.ds(8 * c + 4, 4)], Gv.at[1 - p, pl.ds(8 * c + 4, 4)], G_CUT, cut)
    g_core = rc(Gv.at[p, pl.ds(8 * c, 8)], Gv.at[p, pl.ds(8 * c, 8)], G_CORE, core)
    g_core_in = rc(Gv.at[p, pl.ds(8 * (1 - c), 8)], Gv.at[p, pl.ds(8 * (1 - c), 8)], G_CORE, core)
    g_core2 = rc(Gv.at[1 - p, pl.ds(8 * c, 4)], Gv.at[1 - p, pl.ds(8 * c, 4)], G_CORE2, core)
    g_core2_in = rc(Gv.at[1 - p, pl.ds(8 * (1 - c), 4)], Gv.at[1 - p, pl.ds(8 * (1 - c), 4)], G_CORE2, core)
    g_core3 = rc(Gv.at[1 - p, pl.ds(8 * c + 4, 4)], Gv.at[1 - p, pl.ds(8 * c + 4, 4)], G_CORE3, core)
    g_core3_in = rc(Gv.at[1 - p, pl.ds(8 * (1 - c) + 4, 4)], Gv.at[1 - p, pl.ds(8 * (1 - c) + 4, 4)], G_CORE3, core)
    x_half = rc(Xo.at[:, 1 - u], Xp.at[:, 1 - u], X_X, pair)
    x_half_in = rc(Xo.at[:, u], Xp.at[:, u], X_X, pair)
    x_full = rc(Xo, Xp, X_X, pair)

    def axis(stage, h):
        return (z, zdev) if stage == h else (y, ydev)

    def gather(stage, i, k, h):
        e, to = axis(stage, h)
        e = (e, e, (e + 3) % 4, (e + 1) % 4)[i]
        rows = pl.ds(128 * k + (0, 0, 0, 64)[i], (128, 128, 64, 64)[i])
        if stage == 0:
            ref = Wg.at[e, y, h, rows] if h == 0 else Wg.at[z, e, h, rows]
        else:
            ref = Wg.at[:, e, h, rows] if h == 0 else Wg.at[e, :, h, rows]
        return pltpu.make_async_remote_copy(
            ref, ref, ag_s.at[stage, k, h, i], ag_r.at[stage, k, h, i],
            device_id=to((1, 3, 1, 3)[i]), device_id_type=MESH)

    def gather_on(stage, k):
        for h in range(2):
            for i in range(2):
                gather(stage, i, k, h).wait_recv()
                gather(stage, i + 2, k, h).start()

    def gather_end(stage, k):
        for h in range(2):
            for i in (2, 3):
                gather(stage, i, k, h).wait_recv()

    @pl.when(above)
    def _():
        for k in range(8):
            w_x(k).start()

    def gather_begin(k):
        @pl.when(above)
        def _():
            w_x(k).wait_recv()

        for h in range(2):
            for i in range(2):
                gather(0, i, k, h).start()

    def gather_rows(k):
        for h in range(2):
            for i in range(2):
                gather(1, i, k, h).start()

    def unit(k, j):
        t = jnp.where(s == 1, p, 1 - p) if j == 0 else jnp.where(s == 1, 1 - p, p)
        return t, D.at[pl.ds(8 * c + 2 * k, 2), pl.ds(512 * t, 512)]

    def from_core(k, j):
        t = unit(k, j)[0]
        return D.at[pl.ds(8 * (1 - c) + 2 * k, 2), pl.ds(512 * t, 512)]

    def d_cut(k, j):
        ref = unit(k, j)[1]
        return rc(ref, ref, D_CUT + 2 * k + j, cut)

    def d_core(k, j):
        ref = unit(k, j)[1]
        return rc(ref, ref, D_CORE + 2 * k + j, core)

    def d_core_in(k, j):
        ref = from_core(k, j)
        return rc(ref, ref, D_CORE + 2 * k + j, core)

    def d_on(k, j):
        d_cut(k, j).wait_recv()
        d_core(k, j).start()

    def layer_unit(k, j):
        t = unit(k, j)[0]
        for zz in range(4):
            left = jnp.concatenate([Gv[t, 4 * zz + yy] for yy in range(4)], axis=1)
            right = jnp.concatenate(
                [Wg[zz, yy, h, pl.ds(256 * k, 256), :] for yy in range(4) for h in range(2)], axis=1)
            part = dot_nt(left, right)
            acc[...] = part if zz == 0 else acc[...] + part
        for rr in range(2):
            mine = [Gv[t, 8 * c + 4 * rr + a, :, pl.ds(128 * u, 128)].astype(F32) for a in range(4)]
            mine = merge(mine, lambda a: k)
            D[8 * c + 2 * k + rr, pl.ds(512 * t, 512)] = (acc[:, 128 * rr : 128 * rr + 128] + mine).astype(BF)
        d_cut(k, j).start()

    LOW, HIGH, ALL = pl.ds(0, 128), pl.ds(128, 128), pl.ds(0, 256)

    def block(stage, m, h, e, rows):
        if stage == 1:
            return T.at[m, h, e, rows]
        return S.at[m, e, :, h, rows] if h == 0 else S.at[m, :, e, h, rows]

    def reduce(stage, i, m, h):
        e, to = axis(stage, h)
        rows = (LOW, HIGH, HIGH, LOW, LOW, HIGH)[i]
        src = block(stage, m, h, (e + (2, 2, 1, 3, 1, 3)[i]) % 4, rows)
        first, second = ((Ra, Rb), (Rc, Rd))[stage]
        if i < 2:
            dst = first.at[m, h, i]
        else:
            dst = second.at[m, h, i % 2, :, rows] if stage == 0 else second.at[m, h, i % 2, rows]
        return pltpu.make_async_remote_copy(
            src, dst, rs_s.at[stage, m, h, i], rs_r.at[stage, m, h, i],
            device_id=to((1, 3)[i % 2]), device_id_type=MESH)

    def reduce_start(stage, m, h):
        for i in range(4):
            reduce(stage, i, m, h).start()

    def reduce_on(stage, m):
        for h in range(2):
            e = axis(stage, h)[0]
            for i in range(2):
                reduce(stage, i, m, h).wait_recv()
                mine = block(stage, m, h, (e + (1, 3)[i]) % 4, (LOW, HIGH)[i])
                came = (Ra, Rc)[stage].at[m, h, i]
                if stage == 0:
                    @pl.loop(0, 4)
                    def _(b):
                        mine[b] = (mine[b].astype(F32) + came[b].astype(F32)).astype(BF)
                else:
                    mine[...] = (mine[...].astype(F32) + came[...].astype(F32)).astype(BF)
                reduce(stage, i + 4, m, h).start()

    def row_sums(m):
        for h in range(2):
            for i in range(2, 6):
                reduce(0, i, m, h).wait_recv()
            mine = block(0, m, h, axis(0, h)[0], ALL)

            @pl.loop(0, 4)
            def _(b):
                v = mine[b].astype(F32) + Rb[m, h, 0, b].astype(F32) + Rb[m, h, 1, b].astype(F32)
                T[m, h, b] = v.astype(BF)

                @pl.when(b == axis(1, h)[0])
                def _():
                    Tf[m, h] = v

            reduce_start(1, m, h)

    def f_x(m):
        rows = pl.ds(2 * m, 2)
        return rc(F.at[1 - p, rows], Fp.at[rows], F_X + m, pair)

    def finish(m):
        for h in range(2):
            for i in range(2, 6):
                reduce(1, i, m, h).wait_recv()
            v = Tf[m, h] + Rd[m, h, 0].astype(F32) + Rd[m, h, 1].astype(F32)
            F[h, 2 * m] = v[:128]
            F[h, 2 * m + 1] = v[128:]
            Nb[0, 0] = Nb[0, 0] + jnp.sum((v * v).reshape(32, 8, 128), axis=0)

        @pl.when(above)
        def _():
            f_x(m).start()

    def input_part(n, t, to):
        for zz in range(4):
            left = jnp.concatenate([Gv[t, 8 + 2 * zz], Gv[t, 9 + 2 * zz]], axis=1)
            right = jnp.concatenate(
                [Wg[zz, yy, n // 4, pl.ds(256 * (n % 4), 256), :] for yy in range(4)], axis=1)
            part = dot_nt(left, right)
            to[...] = part if zz == 0 else to[...] + part
        lanes = pl.ds(128 * p, 128)
        mine = Gv[t, 8 + 4 * c + n // 2, :, pl.ds(pl.multiple_of(128 * (n % 2), 128), 128)]
        to[:, lanes] = to[:, lanes] + mine.astype(F32)

    def p_x(i):
        return rc(Gv.at[0, pl.ds(2 * i, 2)], Gv.at[1, pl.ds(2 * i, 2)], P_X + i, pair)

    def weight_grad(m):
        @pl.loop(0, 16)
        def _(q):
            v = dot_nn(XT[pl.ds(256 * m, 256), 0:512], Gv[0, q])
            v = v + dot_nn(XT[pl.ds(256 * m, 256), 512:1024], Gv[1, q])
            S[m, q // 4, q % 4, 0] = v[:, :128].astype(BF)
            S[m, q // 4, q % 4, 1] = v[:, 128:].astype(BF)

    def weight_grad_part(k):
        @pl.loop(0, 4)
        def _(i):
            cc, half = i // 2, i % 2
            right = jnp.concatenate([D[8 * cc + 2 * k], D[8 * cc + 2 * k + 1]], axis=1)
            v = [dot_nn(XT[pl.ds(512 * g + 256 * half, 256), 0:1024], right) for g in range(4)]
            for rr in range(2):
                for a, b in enumerate(transpose([x[:, 128 * rr : 128 * rr + 128] for x in v])):
                    S[k, 2 * cc + rr, a, half] = b.astype(BF)

    def weight_grad_from(k):
        @pl.when(k < 2)
        def _():
            d_core_in(k, 0).wait_recv()

        d_core_in(k, 1).wait_recv()
        weight_grad_part(k)
        first_reduce(k)

    def natural(t):
        @pl.loop(0, 4)
        def _(i):
            b = 8 * (i // 2) + i % 2
            v = transpose([D[b + 2 * g, pl.ds(512 * t, 512)].astype(F32) for g in range(4)])
            for a in range(4):
                Gv[t, 8 + 2 * i + a // 2, :, 128 * (a % 2) : 128 * (a % 2) + 128] = v[a].astype(BF)

    def partner_part(i):
        @pl.loop(0, 2)
        def _(j):
            input_part(2 * i + j, 1 - p, acc)
            Gv[0, 2 * i + j] = acc[...].astype(BF)

    def first_reduce(m):
        for h in range(2):
            reduce_start(0, m, h)

    gather_begin(0)

    @pl.when(above)
    def _():
        for i in range(8):
            gload(i, Gv.at[p, 8 * c + i]).wait()
        g_x.start()
        g_core.start()

    @pl.when(below)
    def _():
        for i in range(4, 8):
            gload(i, Gv.at[0, 8 + i]).wait()
        g_cut.start()

    gather_begin(1)

    @pl.loop(0, 12)
    def _(i):
        @pl.when(i < 6)
        def _():
            gather_begin(i + 2)

        @pl.when(i < 8)
        def _():
            gather_on(0, i)

        @pl.when((i >= 1) & (i < 9))
        def _():
            gather_end(0, i - 1)
            gather_rows(i - 1)

        @pl.when((i >= 3) & (i < 11))
        def _():
            gather_on(1, i - 3)

        @pl.when(i >= 4)
        def _():
            gather_end(1, i - 4)

        @pl.when(i == 4)
        def _():
            for j in range(16):
                xload(j).wait()

            @pl.when(below)
            def _():
                x_full.start()

                @pl.loop(0, 16)
                def _(j):
                    XT[pl.ds(128 * j, 128), pl.ds(512 * p, 512)] = Xo[j // 2, j % 2].T

            @pl.when(above)
            def _():
                g_core_in.wait_recv()

                @pl.loop(0, 8)
                def _(r):
                    XT[pl.ds(128 * r, 128), pl.ds(512 * p, 512)] = Xo[r, u].T

        @pl.when(above & (i >= 5) & (i % 2 == 1))
        def _():
            k = (i - 5) // 2
            layer_unit(k, 0)

            @pl.when(k == 0)
            def _():
                g_x_in.wait_recv()
                g_core2.start()
                x_half.start()
                g_cut_in.wait_recv()
                g_core3.start()
                g_core2_in.wait_recv()
                g_core3_in.wait_recv()

            @pl.when(k < 2)
            def _():
                layer_unit(k, 1)

        @pl.when(above & (i == 10))
        def _():
            x_half_in.wait_recv()

            @pl.loop(0, 8)
            def _(r):
                XT[pl.ds(128 * r, 128), pl.ds(512 * (1 - p), 512)] = Xp[r, u].T

            weight_grad(0)
            first_reduce(0)

        @pl.when(below & ((i == 9) | (i == 11)))
        def _():
            d_on((i - 9) // 2, 0)
            d_on((i - 9) // 2, 1)

        @pl.when(below & (i == 10))
        def _():
            x_full.wait_recv()

            @pl.loop(0, 16)
            def _(j):
                XT[pl.ds(128 * j, 128), pl.ds(512 * (1 - p), 512)] = Xp[j // 2, j % 2].T

        @pl.when(below & (i >= 10))
        def _():
            weight_grad_from(i - 10)

    @pl.when(above)
    def _():
        @pl.loop(2, 4)
        def _(k):
            layer_unit(k, 1)

        rc(D.at[pl.ds(8 * c, 8), pl.ds(512 * (1 - p), 512)], Dp, O_X, pair).start()
    @pl.when(below)
    def _():
        g_cut.wait_send()

        @pl.loop(2, 4)
        def _(k):
            d_on(k, 0)

        @pl.loop(2, 4)
        def _(k):
            d_core_in(k, 0).wait_recv()

        natural(1 - p)

        partner_part(0)
        p_x(0).start()
        reduce_on(0, 0)

        @pl.loop(2, 4)
        def _(k):
            d_on(k, 1)
            weight_grad_from(k)
            partner_part(k - 1)
            p_x(k - 1).start()

            @pl.when(k == 2)
            def _():
                reduce_on(0, 1)

        row_sums(0)
        partner_part(3)
        p_x(3).start()

        natural(p)

    Nb[0, 0] = jnp.zeros((8, 128), F32)

    @pl.loop(0, 8)
    def _(i):
        @pl.when(above & (i >= 1) & (i < 4))
        def _():
            weight_grad(i)
            first_reduce(i)

        @pl.when((i >= 1) & (i < 5) & (above | (i >= 3)))
        def _():
            reduce_on(0, i - 1)

        @pl.when((i >= 2) & (i < 6) & (above | (i >= 3)))
        def _():
            row_sums(i - 2)

        @pl.when((i >= 3) & (i < 7))
        def _():
            reduce_on(1, i - 3)

        @pl.when(i >= 4)
        def _():
            finish(i - 4)

        @pl.when(below & (i >= 2) & (i < 6))
        def _():
            for j in range(2):
                input_part(2 * (i - 2) + j, p, Own.at[2 * (i - 2) + j])

    def own_part(i):
        @pl.when(below)
        def _():
            p_x(i).wait_recv()
            for n in (2 * i, 2 * i + 1):
                out_ref[:, 256 * n : 256 * n + 256] = (Own[n] + Gv[1, n].astype(F32)).astype(BF)

    steps = [near, [ydev(1), ydev(3), ydev(2)], [zdev(1), zdev(3), zdev(2)]]
    for i, targets in enumerate(steps):
        copies = [
            pltpu.make_async_remote_copy(
                Nb.at[i, 0], Nb.at[i, j + 1], ns.at[i, j], nr.at[i, j], device_id=to, device_id_type=MESH)
            for j, to in enumerate(targets)]
        for copy in copies:
            copy.start()
        for copy in copies:
            copy.wait_recv()
        v = Nb[i, 0]
        for j in range(len(targets)):
            v = v + Nb[i, j + 1]
        if i + 1 < len(steps):
            Nb[i + 1, 0] = v
        else:
            total = v
        for copy in copies:
            copy.wait_send()
    total = jnp.broadcast_to(jnp.sum(total, keepdims=True), (8, 128))
    clip = jnp.minimum(1.0, 1.0 / (jnp.sqrt(total / 33554432.0) + 1e-06))[0:1, :]

    @pl.when(above)
    def _():
        for m in range(4):
            f_x(m).wait_recv()
        for r in range(8):
            grad_ref[pl.ds(256 * r + 128 * u, 128), :] = F[p, r] * clip
            grad_ref[pl.ds(256 * r + 128 * (1 - u), 128), :] = Fp[r] * clip

    @pl.when(below)
    def _():
        for r in range(4):
            half, low = r // 2, r % 2
            v = transpose([F[half, 2 * k + low] for k in range(4)])
            for g in range(4):
                rows = 512 * g + 256 * half + 128 * low
                grad_ref[rows : rows + 128, :] = v[g] * clip

    for i in range(4):
        own_part(i)

    @pl.when(above)
    def _():
        rc(Dp, Dp, O_X, pair).wait_recv()

        @pl.loop(0, 2)
        def _(i):
            for par, src in ((u, D.at[pl.ds(8 * c, 8), pl.ds(512 * p, 512)]), (1 - u, Dp)):
                v = transpose([src[2 * g + i].astype(F32) for g in range(4)])
                for a in range(4):
                    lanes = pl.ds(pl.multiple_of(1024 * i + 256 * a + 128 * par, 128), 128)
                    out_ref[:, lanes] = v[a].astype(BF)

    @pl.loop(0, 8)
    def _(k):
        for h in range(2):
            for stage in range(2):
                for i in range(4):
                    gather(stage, i, k, h).wait_send()

    @pl.loop(0, 4)
    def _(k):
        for h in range(2):
            for stage in range(2):
                for i in range(6):
                    reduce(stage, i, k, h).wait_send()

    @pl.when(above)
    def _():
        for copy in (g_x, g_core, g_core2, g_core3, x_half):
            copy.wait_send()
        for m in range(4):
            f_x(m).wait_send()
        for k in range(8):
            w_x(k).wait_send()
        rc(Dp, Dp, O_X, pair).wait_send()

        @pl.loop(0, 4)
        def _(k):
            d_cut(k, 0).wait_send()
            d_cut(k, 1).wait_send()

    @pl.when(below)
    def _():
        x_full.wait_send()

        @pl.loop(0, 4)
        def _(k):
            d_core(k, 0).wait_send()
            d_core(k, 1).wait_send()

        for i in range(4):
            p_x(i).wait_send()


def per_device(saved_input, out_grad, master_weight, moment1, moment2):
    vmem = pl.BlockSpec(memory_space=pltpu.VMEM)
    hbm = pl.BlockSpec(memory_space=pl.ANY)
    dma = pltpu.SemaphoreType.DMA
    input_grad, clipped = pl.pallas_call(
        kernel,
        out_shape=(
            jax.ShapeDtypeStruct((512, 2048), BF),
            jax.ShapeDtypeStruct((2048, 128), F32),
        ),
        in_specs=[hbm, hbm, vmem],
        out_specs=(vmem, vmem),
        scratch_shapes=[
            pltpu.VMEM((4, 4, 2, 1024, 128), BF),
            pltpu.VMEM((1024, 128), BF),
            pltpu.VMEM((2, 16, 512, 256), BF),
            pltpu.VMEM((16, 1024, 128), BF),
            pltpu.VMEM((8, 512, 128), BF),
            pltpu.VMEM((8, 2, 512, 128), BF),
            pltpu.VMEM((8, 2, 512, 128), BF),
            pltpu.VMEM((2048, 1024), BF),
            pltpu.VMEM((4, 4, 4, 2, 256, 128), BF),
            pltpu.VMEM((4, 2, 2, 4, 128, 128), BF),
            pltpu.VMEM((4, 2, 2, 4, 256, 128), BF),
            pltpu.VMEM((4, 2, 2, 128, 128), BF),
            pltpu.VMEM((4, 2, 2, 256, 128), BF),
            pltpu.VMEM((4, 2, 4, 256, 128), BF),
            pltpu.VMEM((4, 2, 256, 128), F32),
            pltpu.VMEM((2, 8, 128, 128), F32),
            pltpu.VMEM((8, 128, 128), F32),
            pltpu.VMEM((512, 256), F32),
            pltpu.VMEM((8, 512, 256), F32),
            pltpu.VMEM((3, 8, 8, 128), F32),
            dma((16,)), dma((8,)),
            dma((2, 8, 2, 4)), dma((2, 8, 2, 4)),
            dma((2, 4, 2, 6)), dma((2, 4, 2, 6)),
            dma((39,)), dma((39,)),
            dma((3, 7)), dma((3, 7)),
        ],
        compiler_params=pltpu.CompilerParams(
            collective_id=0, has_side_effects=True, vmem_limit_bytes=62 * 2**20),
    )(saved_input.reshape(512, 2048), out_grad.reshape(512, 2048), master_weight[0])
    master = master_weight[0]
    new_moment1 = 0.9 * moment1[0] + 0.1 * clipped
    new_moment2 = 0.95 * moment2[0] + 0.05 * clipped * clipped
    first_fix = 1.0 - 0.9**10
    second_fix = 1.0 - 0.95**10
    update = new_moment1 / first_fix / (jnp.sqrt(new_moment2 / second_fix) + 1e-08)
    new_weight = master - 0.01 * (update + 0.1 * master)
    return (input_grad.reshape(1, 2, 256, 2048), new_weight[None], new_moment1[None], new_moment2[None])


def solution(mesh):
    return jax.shard_map(
        per_device,
        mesh=mesh,
        in_specs=(
            P("section", None, "dp", "mp"),
            P(None, "dp", "mp"),
            P("section", "mp", "dp"),
            P("section", "mp", "dp"),
            P("section", "mp", "dp"),
        ),
        out_specs=(
            P("section", None, "dp", "mp"),
            P("section", "mp", "dp"),
            P("section", "mp", "dp"),
            P("section", "mp", "dp"),
        ),
        check_vma=False,
    )
```
